512 devices in a mesh: expert: 64 (over y, z), hidden: 8 (over x, core).
Axes of the slice: x: 4, y: 4, z: 16, core: 2. Of those that a mesh axis runs over, the one named last changes fastest.
Arguments:
- tokens: bfloat16 [4096, 4096], P('expert', 'hidden'), may hold values from -6 to 6
- route_ids: int32 [4096, 8], P('expert'), may hold values from 0 to 63, all different within a row; in each aligned block of 64 rows (0 to 63, 64 to 127, ...) at most 12 rows name the same one
- route_weights: float32 [4096, 8], P('expert'), may hold values from 0.05 to 1
- gate_up: bfloat16 [64, 2, 768, 4096], P('expert', None, 'hidden'), may hold values from -0.09375 to 0.09375
- down_proj: bfloat16 [64, 768, 4096], P('expert', None, 'hidden'), may hold values from -0.21875 to 0.21875
Outputs:
- layer_out: bfloat16 [4096, 4096], P('expert', 'hidden')
- hessian: float32 [64, 768, 768], P('expert', 'hidden')
The draws below stay inside these ranges and needn't reach their ends.
Inputs may be any that keep to these rules, and one draw needn't show every extreme that they name: `route_ids`: each token names 8 different experts. Within the rows of one device (aligned blocks of 64 tokens) no expert is named more than 12 times, and in some block one expert is named exactly 12 times. Every expert is named by some token.
All inputs are finite; a program needn't handle non-finite values.
Results may differ from the reference program's by a relative error of at most 0.012.
Values may be sent and summed in bfloat16 or wider, within the bound.
No kernel may reach another device: no remote copies, remote signals or barrier semaphores. Data moves between devices by JAX's collectives and lax.ppermute only.
A program may use at most 64 MiB of HBM per device.

```python
import math
import jax
import jax.numpy as jnp
import numpy as np
from jax import lax

D = 4096
FF = 768
TOP = 8
TOK_DEV = 64
EXPERTS = 64
TOKENS = 4096
CAP = 12
N_EXPERT = 64


def block_levels(rng, shape, pieces, smallest, largest):
    def one(dim, blocks):
        draws = jax.random.uniform(jax.random.fold_in(jax.random.fold_in(rng, 6), dim), (blocks,), jnp.float32, smallest / len(pieces), largest / len(pieces))
        return jnp.repeat(jnp.exp(draws), shape[dim] // blocks).reshape((-1,) + (1,) * (len(shape) - dim - 1))

    gain = one(*pieces[0])
    for cut in pieces[1:]:
        gain = gain * one(*cut)
    return gain


def deal_out(stream_key, own, number, rows, number_of, top, limit, skew):
    ranking = jax.random.permutation(stream_key, number_of)
    crowded, usual = shares(number_of, rows * top, limit, skew, True), shares(number_of, rows * top, limit, skew, False)
    places = jnp.arange(number_of)

    def named(tallies, offset_by):
        used = int((tallies > 0).sum())
        fixed = max(1, used // 4)
        passed = fixed + (places - fixed + offset_by * (used - fixed)) % max(1, number_of - fixed)
        return jnp.zeros((number_of,), jnp.int32).at[ranking[jnp.where(places < fixed, places, passed)]].set(jnp.asarray(tallies, jnp.int32))

    tallies = jnp.where(number % 4 == 0, named(crowded, number // 4), named(usual, number - number // 4 - 1))
    mixed = jax.random.permutation(jax.random.fold_in(own, 3), number_of)
    donor, taker = mixed[0:number_of // 2 * 2:2], mixed[1:number_of // 2 * 2:2]
    slack = jnp.minimum(tallies[donor] - 1, limit - tallies[taker]) // 2
    slack = jnp.where((donor == ranking[0]) | (taker == ranking[0]) | (tallies[taker] == 0), 0, jnp.maximum(slack, 0))
    passed = jax.random.randint(jax.random.fold_in(own, 4), (number_of // 2,), 0, 1 << 20) % (slack + 1)
    tallies = tallies.at[donor].add(-passed).at[taker].add(passed)
    labels = jnp.searchsorted(jnp.cumsum(tallies), jnp.arange(rows * top), side="right").astype(jnp.int32)
    listing = labels.reshape(top, rows).T
    listing = listing[jax.random.permutation(jax.random.fold_in(own, 1), rows)]
    offset_by = jax.random.randint(jax.random.fold_in(own, 2), (rows, 1), 0, top)
    return jnp.take_along_axis(listing, (jnp.arange(top)[None, :] + offset_by) % top, axis=1)


def shares(amount, total, limit, skew, full):
    weights = [(1 << 20) // math.isqrt(rank ** skew) + 1 for rank in range(1, amount + 1)]
    largest = limit if full else min(limit, max(-(-total // amount), total * weights[0] // sum(weights)))
    least = 1 if total - largest >= amount - 1 else 0
    counts, spare = [largest] + [least] * (amount - 1), total - largest - least * (amount - 1)
    while spare > 0:
        movable = [i for i in range(1, amount) if counts[i] < largest] or [i for i in range(1, amount) if counts[i] < limit]
        whole, remaining = sum([weights[i] for i in movable]), spare
        for i in movable:
            addition = min(limit - counts[i], max(1, remaining * weights[i] // whole), spare)
            counts[i] = counts[i] + addition
            spare = spare - addition
    return np.array(counts)


def gaussian(key, extent, deviation, bound, split=(), kind=jnp.bfloat16):
    level = block_levels(key, extent, split, -0.22, 0.18) if split else 1.0
    drawn = jax.random.normal(key, extent, jnp.float32) * deviation * level
    return jnp.minimum(jnp.maximum(drawn, -bound), bound).astype(kind)


def setup_inputs(seed: int = 0) -> dict:
    key_of = jax.random.split(jax.random.key(seed), 6)
    tokens = gaussian(key_of[0], (TOKENS, D), 1.0, 6.0, ((0, 64), (1, 8)))
    route_ids_keys = jax.random.split(jax.random.fold_in(key_of[1], 1), TOKENS // TOK_DEV)
    route_ids_turns = jax.random.permutation(jax.random.fold_in(key_of[1], 3), TOKENS // TOK_DEV)
    route_ids = jax.vmap(lambda own, number: deal_out(jax.random.fold_in(key_of[1], 2), own, number, TOK_DEV, EXPERTS, TOP, CAP, 2))(route_ids_keys, route_ids_turns).reshape((TOKENS, TOP))
    route_weights = jnp.clip(jnp.exp(math.log(1.0) - 2.9957323 * jax.random.uniform(key_of[2], (TOKENS, TOP), jnp.float32) ** block_levels(key_of[2], (TOKENS, TOP), ((0, 64),), -0.2, 0.2)), 0.05, 1.0)
    gate_up = gaussian(key_of[3], (EXPERTS, 2, FF, D), D ** -0.5, 0.09375, ((0, 64), (2, 8)))
    down_proj = gaussian(key_of[4], (EXPERTS, FF, D), FF ** -0.5, 0.21875, ((0, 64), (2, 8)))
    return {"tokens": tokens, "route_ids": route_ids, "route_weights": route_weights, "gate_up": gate_up, "down_proj": down_proj}


def reference(tokens, route_ids, route_weights, gate_up, down_proj):
    slots_all = N_EXPERT * CAP
    flat_ids = route_ids.reshape(-1).astype(jnp.int32)
    route_share = route_weights / jnp.sum(route_weights, axis=1, keepdims=True)
    flat_share = route_share.reshape(-1)
    positions = jnp.arange(slots_all, dtype=jnp.int32)

    def one_expert(layer_acc, inputs):
        expert, weight_pair, weight_down = inputs
        chosen = flat_ids == expert
        number = jnp.sum(chosen.astype(jnp.int32))
        routes = jnp.nonzero(chosen, size=slots_all, fill_value=0)[0].astype(jnp.int32)
        live_rows = positions < number
        token_rows = (routes // TOP).astype(jnp.int32)
        gathered = jnp.where(live_rows[:, None], tokens[token_rows], jnp.zeros((), jnp.bfloat16))
        gate_val = jnp.dot(gathered, weight_pair[0].T, preferred_element_type=jnp.float32)
        upward = jnp.dot(gathered, weight_pair[1].T, preferred_element_type=jnp.float32)
        hidden = (jax.nn.silu(gate_val) * upward).astype(jnp.bfloat16)
        gram_block = jnp.dot(hidden.T, hidden, preferred_element_type=jnp.float32) * (2.0 / number.astype(jnp.float32))
        expert_out = jnp.dot(hidden, weight_down, preferred_element_type=jnp.float32).astype(jnp.bfloat16)
        weights_live = jnp.where(live_rows, flat_share[routes], 0.0)
        contrib = weights_live[:, None] * expert_out.astype(jnp.float32)
        layer_acc = layer_acc.at[token_rows].add(contrib)
        return layer_acc, gram_block

    start_acc = jnp.zeros((tokens.shape[0], tokens.shape[1]), jnp.float32)
    experts_idx = jnp.arange(EXPERTS, dtype=jnp.int32)
    layer_acc, hessian = lax.scan(one_expert, start_acc, (experts_idx, gate_up, down_proj))
    return layer_acc.astype(jnp.bfloat16), hessian
```

```python
import jax
import jax.numpy as jnp
from jax import lax
from jax.experimental import pallas as pl
from jax.experimental.pallas import tpu as pltpu
from jax.sharding import PartitionSpec as P

BF = jnp.bfloat16
F32 = jnp.float32
I32 = jnp.int32

TOK = 64
TOP = 8
EXPERTS = 64
CAP = 12
LANES = 128
SLABS = 4
PACK = SLABS * CAP
GROUP = 8
GROWS = GROUP * CAP
GPACK = GROUP * PACK
CHIPS = 4
ROWS = EXPERTS * CAP
UNITS = 96
EMPTY = 64.0
NT = (((1,), (1,)), ((), ()))
TN = (((0,), (0,)), ((), ()))


def dot(a, b, dims=(((1,), (0,)), ((), ()))):
    return lax.dot_general(a, b, dims, preferred_element_type=F32)


def iota(shape, dim):
    return lax.broadcasted_iota(I32, shape, dim)


def codes(ids, shares=None):
    wide = SLABS * TOK
    expert = iota((EXPERTS, wide), 0)
    member = jnp.zeros((EXPERTS, wide), F32)
    weight = jnp.zeros((EXPERTS, wide), F32)
    for k in range(TOP):
        hit = ids[k : k + 1, :] == expert
        member = member + jnp.where(hit, 1.0, 0.0)
        if shares is not None:
            weight = weight + jnp.where(hit, shares[k : k + 1, :], 0.0)
    row, col = iota((wide, wide), 0), iota((wide, wide), 1)
    before = jnp.where((row < TOK) & (row < (col & (TOK - 1))), 1.0, 0.0).astype(BF)
    slot = dot(member.astype(BF), before)
    slab = (iota((EXPERTS, wide), 1) >> 6).astype(F32)
    code = jnp.where(member > 0.5, slot + 16.0 * slab, -1.0)
    return code, member, weight


def pack_kernel(tok_ref, ids_ref, out_ref):
    code, member, _ = codes(ids_ref[...])
    wide = SLABS * TOK
    ones = jnp.where(iota((wide, LANES), 0) < TOK, 1.0, 0.0).astype(BF)
    count = dot(member.astype(BF), ones)
    tok = tok_ref[...]
    slabs = jnp.concatenate([tok[:, l * LANES : (l + 1) * LANES] for l in range(SLABS)], axis=0)
    p = iota((PACK, wide), 0)
    slab = (p >= CAP).astype(I32) + (p >= 2 * CAP).astype(I32) + (p >= 3 * CAP).astype(I32)
    target = (p + 4 * slab).astype(F32)
    q = iota((PACK, LANES), 0)
    first = jnp.where(q < CAP, q, -1).astype(F32)
    for c in range(EXPERTS // GROUP):
        picks = [
            jnp.where(code[e : e + 1, :] == target, 1.0, 0.0).astype(BF)
            for e in range(c * GROUP, (c + 1) * GROUP)
        ]
        rows = dot(jnp.concatenate(picks, axis=0), slabs)
        for j in range(GROUP):
            e = c * GROUP + j
            block = rows[j * PACK : (j + 1) * PACK]
            out_ref[e] = jnp.where(first >= count[e : e + 1, :], EMPTY, block).astype(BF)


def unpack_matrix():
    out, src = iota((GPACK, GPACK), 0), iota((GPACK, GPACK), 1)
    l, rest = out // GROWS, out % GROWS
    return jnp.where(src == (rest // CAP) * PACK + l * CAP + rest % CAP, 1.0, 0.0).astype(BF)


def up_kernel(place_ref, a_ref, b_ref, w0_ref, w1_ref, w2_ref, w3_ref, perm_ref, out_ref, scale_ref, wa, wb):
    x, c = place_ref[0], place_ref[1]
    half = SLABS * LANES
    own = pl.multiple_of(c * half, half)
    other = pl.multiple_of((1 - c) * half, half)
    for k, w_ref in enumerate((w0_ref, w1_ref, w2_ref, w3_ref)):
        at = pl.multiple_of(((x + CHIPS - k) % CHIPS) * UNITS, 32)
        for g in range(2):
            wa[pl.ds(at + g * CHIPS * UNITS, UNITS), :] = w_ref[g * UNITS : (g + 1) * UNITS, pl.ds(own, half)]
            wb[pl.ds(at + g * CHIPS * UNITS, UNITS), :] = w_ref[g * UNITS : (g + 1) * UNITS, pl.ds(other, half)]
    perm = perm_ref[...]
    empty = jnp.zeros((GROWS, LANES), F32)

    def rows_of(block, empty):
        y = dot(perm, block.reshape(GPACK, LANES))
        first = y[:GROWS]
        gone = first > 0.5 * EMPTY
        empty = empty + jnp.where(gone, 1.0, 0.0)
        parts = [jnp.where(gone, 0.0, first)] + [y[l * GROWS : (l + 1) * GROWS] for l in range(1, SLABS)]
        return jnp.concatenate([part.astype(BF) for part in parts], axis=1), empty

    for g in range(EXPERTS // GROUP):
        own_rows, empty = rows_of(a_ref[g * GROUP : (g + 1) * GROUP], empty)
        other_rows, _ = rows_of(b_ref[g * GROUP : (g + 1) * GROUP], empty)
        part = dot(own_rows, wa[...], NT) + dot(other_rows, wb[...], NT)
        out_ref[g // 2, (g % 2) * GROWS : (g % 2 + 1) * GROWS, :] = part.astype(BF)
    gone = jnp.sum(empty, axis=0, keepdims=True)
    scale_ref[...] = jnp.broadcast_to(2.0 / (float(ROWS) - gone), scale_ref.shape)


def silu_kernel(in_ref, out_ref):
    total = in_ref[0].astype(F32)
    for k in range(1, CHIPS):
        total = total + in_ref[k].astype(F32)
    half = CHIPS * UNITS
    gate, up = total[:, :half], total[:, half:]
    out_ref[...] = (gate / (1.0 + jnp.exp(-gate)) * up).astype(BF)


def down_kernel(place_ref, own_ref, other_ref, down_ref, perm_ref, out_ref, da, db):
    c = place_ref[1]
    for i in range(CHIPS):
        mine = pl.multiple_of((2 * i + c) * UNITS, 32)
        theirs = pl.multiple_of((2 * i + 1 - c) * UNITS, 32)
        da[i * UNITS : (i + 1) * UNITS, :] = down_ref[pl.ds(mine, UNITS), :]
        db[i * UNITS : (i + 1) * UNITS, :] = down_ref[pl.ds(theirs, UNITS), :]
    perm = perm_ref[...]
    sources = EXPERTS // CHIPS
    for k in range(CHIPS):
        rows = (dot(own_ref[k], da[...]) + dot(other_ref[k], db[...])).astype(BF)
        for h in range(2):
            part = rows[h * GROWS : (h + 1) * GROWS]
            stack = jnp.concatenate([part[:, l * LANES : (l + 1) * LANES] for l in range(SLABS)], axis=0)
            packed = dot(perm, stack, TN).astype(BF).reshape(GROUP, PACK, LANES)
            out_ref[k * sources + h * GROUP : k * sources + (h + 1) * GROUP] = packed


def gram_kernel(place_ref, own_ref, other_ref, scale_ref, out_ref, acc):
    x, c = place_ref[0], place_ref[1]
    half = CHIPS * UNITS
    row, col = iota((half, 2 * half), 0), iota((half, 2 * half), 1)
    even = row + UNITS * (row // UNITS)
    put_own = jnp.where(col == even + UNITS * c, 1.0, 0.0).astype(BF)
    put_other = jnp.where(col == even + UNITS * (1 - c), 1.0, 0.0).astype(BF)
    for k in range(CHIPS):
        own = own_ref[k]
        every = (dot(own, put_own) + dot(other_ref[k], put_other)).astype(BF)
        gram = dot(own, every, TN)
        acc[...] = gram if k == 0 else acc[...] + gram
    mine = acc[pl.ds(pl.multiple_of(x * UNITS, 32), UNITS), :]
    out_ref[...] = mine * scale_ref[0:1, 0:1]


def combine_kernel(ids_ref, weights_ref, in_ref, out_ref):
    weights = weights_ref[...]
    shares = weights / jnp.sum(weights, axis=0, keepdims=True)
    code, _, share = codes(ids_ref[...], shares)
    code, share = code.astype(BF), share.astype(BF)
    total = jnp.zeros((SLABS * TOK, LANES), F32)
    for g in range(EXPERTS // GROUP):
        q = iota((EXPERTS, GPACK), 1)
        e = iota((EXPERTS, GPACK), 0) - g * GROUP
        spread = jnp.where((q >= e * PACK) & (q < (e + 1) * PACK), 1.0, 0.0).astype(BF)
        p = iota((SLABS * TOK, GPACK), 1) % PACK
        slab = (p >= CAP).astype(I32) + (p >= 2 * CAP).astype(I32) + (p >= 3 * CAP).astype(I32)
        target = (p + 4 * slab).astype(F32)
        pick = jnp.where(dot(code, spread, TN) == target, dot(share, spread, TN), 0.0).astype(BF)
        total = total + dot(pick, in_ref[g * GROUP : (g + 1) * GROUP].reshape(GPACK, LANES))
    out_ref[...] = jnp.concatenate(
        [total[l * TOK : (l + 1) * TOK] for l in range(SLABS)], axis=1
    ).astype(BF)


VMEM = pl.BlockSpec(memory_space=pltpu.VMEM)
SMEM = pl.BlockSpec(memory_space=pltpu.SMEM)


def call(kernel, outs, ins, scratch=(), smem=False, flops=0, size=0):
    return pl.pallas_call(
        kernel,
        out_shape=outs,
        in_specs=([SMEM] if smem else []) + [VMEM] * (len(ins) - int(smem)),
        out_specs=jax.tree.map(lambda _: VMEM, outs),
        scratch_shapes=list(scratch),
        compiler_params=pltpu.CompilerParams(vmem_limit_bytes=40 * 1024 * 1024),
        cost_estimate=pl.CostEstimate(flops=flops, bytes_accessed=size, transcendentals=0),
    )(*ins)


def shape(dims, dtype=BF):
    return jax.ShapeDtypeStruct(dims, dtype)


def body(tokens, route_ids, route_weights, gate_up, down_proj):
    place = lax.axis_index("hidden")
    x, c = place // 2, place % 2
    where = jnp.stack([x, c]).astype(I32)
    half = SLABS * LANES
    wide = 2 * half
    groups = [[2 * i + j for i in range(CHIPS)] for j in range(2)]
    swap = [(i, i ^ 1) for i in range(2 * CHIPS)]

    weights = gate_up.reshape(2 * UNITS, CHIPS * wide)
    pieces = []
    for k in range(CHIPS):
        piece = lax.dynamic_slice(weights, (0, ((x + k) % CHIPS) * wide), (2 * UNITS, wide))
        if k:
            piece = lax.ppermute(piece, "hidden", [(i, (i + 2 * k) % (2 * CHIPS)) for i in range(2 * CHIPS)])
        pieces.append(piece)

    ids = jnp.tile(route_ids.T, (1, SLABS))
    shares = jnp.tile(route_weights.T, (1, SLABS))
    perm = unpack_matrix()

    outgoing = call(pack_kernel, shape((EXPERTS, PACK, LANES)), (tokens, ids), flops=2 * 10**8, size=10**6)
    mine = lax.all_to_all(outgoing, "expert", 0, 0)
    theirs = lax.ppermute(mine, "hidden", swap)

    part, scale = call(
        up_kernel,
        (shape((CHIPS, ROWS // CHIPS, 2 * CHIPS * UNITS)), shape((8, LANES), F32)),
        (where, mine, theirs, *pieces, perm),
        (pltpu.VMEM((2 * CHIPS * UNITS, half), BF), pltpu.VMEM((2 * CHIPS * UNITS, half), BF)),
        smem=True,
        flops=2 * 10**9,
        size=5 * 10**6,
    )
    parts = lax.all_to_all(part, "hidden", 0, 0, axis_index_groups=groups)
    hidden = call(silu_kernel, shape((ROWS // CHIPS, CHIPS * UNITS)), (parts,), size=2 * 10**6)

    copies = jnp.broadcast_to(hidden[None], (CHIPS, *hidden.shape))
    own = lax.all_to_all(copies, "hidden", 0, 0, axis_index_groups=groups)
    other = lax.ppermute(own, "hidden", swap)

    returning = call(
        down_kernel,
        shape((EXPERTS, PACK, LANES)),
        (where, own, other, down_proj.reshape(ROWS, half), perm),
        (pltpu.VMEM((CHIPS * UNITS, half), BF), pltpu.VMEM((CHIPS * UNITS, half), BF)),
        smem=True,
        flops=10**9,
        size=4 * 10**6,
    )
    returned = lax.all_to_all(returning, "expert", 0, 0)
    hessian = call(
        gram_kernel,
        shape((UNITS, 2 * CHIPS * UNITS), F32),
        (where, own, other, scale),
        (pltpu.VMEM((CHIPS * UNITS, 2 * CHIPS * UNITS), F32),),
        smem=True,
        flops=2 * 10**9,
        size=3 * 10**6,
    )
    layer_out = call(combine_kernel, shape((TOK, half)), (ids, shares, returned), flops=4 * 10**8, size=10**6)
    return layer_out, hessian[None]


def solution(mesh):
    return jax.shard_map(
        body,
        mesh=mesh,
        in_specs=(
            P("expert", "hidden"),
            P("expert", None),
            P("expert", None),
            P("expert", None, "hidden", None),
            P("expert", None, "hidden"),
        ),
        out_specs=(P("expert", "hidden"), P("expert", "hidden", None)),
        check_vma=False,
    )
```

```python
import jax
import jax.numpy as jnp
from jax import lax
from jax.experimental import pallas as pl
from jax.experimental.pallas import tpu as pltpu
from jax.sharding import PartitionSpec as P

BF = jnp.bfloat16
F32 = jnp.float32
I32 = jnp.int32

TOK = 64
TOP = 8
EXPERTS = 64
CAP = 12
LANES = 128
SLABS = 4
PACK = SLABS * CAP
GROUP = 8
GROWS = GROUP * CAP
GPACK = GROUP * PACK
CHIPS = 4
ROWS = EXPERTS * CAP
UNITS = 96
EMPTY = 64.0
NT = (((1,), (1,)), ((), ()))
TN = (((0,), (0,)), ((), ()))


def dot(a, b, dims=(((1,), (0,)), ((), ()))):
    return lax.dot_general(a, b, dims, preferred_element_type=F32)


def iota(shape, dim):
    return lax.broadcasted_iota(I32, shape, dim)


def codes(ids, shares=None):
    wide = SLABS * TOK
    copies = jnp.where((iota((TOK, wide), 1) & (TOK - 1)) == iota((TOK, wide), 0), 1.0, 0.0).astype(BF)
    ids = dot(ids.astype(F32).astype(BF), copies).astype(I32)
    if shares is not None:
        shares = dot(shares.astype(BF), copies)
    expert = iota((EXPERTS, wide), 0)
    member = jnp.zeros((EXPERTS, wide), F32)
    weight = jnp.zeros((EXPERTS, wide), F32)
    for k in range(TOP):
        hit = ids[k : k + 1, :] == expert
        member = member + jnp.where(hit, 1.0, 0.0)
        if shares is not None:
            weight = weight + jnp.where(hit, shares[k : k + 1, :], 0.0)
    row, col = iota((wide, wide), 0), iota((wide, wide), 1)
    before = jnp.where((row < TOK) & (row < (col & (TOK - 1))), 1.0, 0.0).astype(BF)
    slot = dot(member.astype(BF), before)
    slab = (iota((EXPERTS, wide), 1) >> 6).astype(F32)
    code = jnp.where(member > 0.5, slot + 16.0 * slab, -1.0)
    return code, member, weight


def pack_kernel(tok_hbm, ids_hbm, out_ref, tok_ref, ids_ref, tok_sem, ids_sem):
    fetch_ids = pltpu.make_async_copy(ids_hbm, ids_ref, ids_sem)
    fetch_ids.start()
    fetch = pltpu.make_async_copy(tok_hbm, tok_ref, tok_sem)
    fetch.start()
    fetch_ids.wait()
    code, member, _ = codes(ids_ref[...])
    wide = SLABS * TOK
    ones = jnp.where(iota((wide, LANES), 0) < TOK, 1.0, 0.0).astype(BF)
    count = dot(member.astype(BF), ones)
    fetch.wait()
    tok = tok_ref[...]
    slabs = jnp.concatenate([tok[:, l * LANES : (l + 1) * LANES] for l in range(SLABS)], axis=0)
    p = iota((PACK, wide), 0)
    slab = (p >= CAP).astype(I32) + (p >= 2 * CAP).astype(I32) + (p >= 3 * CAP).astype(I32)
    target = (p + 4 * slab).astype(F32)
    q = iota((PACK, LANES), 0)
    first = jnp.where(q < CAP, q, -1).astype(F32)
    for c in range(EXPERTS // GROUP):
        picks = [
            jnp.where(code[e : e + 1, :] == target, 1.0, 0.0).astype(BF)
            for e in range(c * GROUP, (c + 1) * GROUP)
        ]
        rows = dot(jnp.concatenate(picks, axis=0), slabs)
        for j in range(GROUP):
            e = c * GROUP + j
            block = rows[j * PACK : (j + 1) * PACK]
            out_ref[e] = jnp.where(first >= count[e : e + 1, :], EMPTY, block).astype(BF)


def repack_matrix(packs):
    loose = iota((GPACK, LANES), 0)
    slab = sum((loose >= l * GROWS).astype(I32) for l in range(1, SLABS))
    rest = loose - slab * GROWS
    source = sum((rest >= j * CAP).astype(I32) for j in range(1, GROUP))
    place = source * (PACK - CAP) + slab * CAP + rest
    parts = [
        jnp.where(place == iota((GPACK, LANES), 1) + j * LANES, 1.0, 0.0) for j in range(GPACK // LANES)
    ]
    matrix = jnp.concatenate(parts, axis=1)
    return (matrix.T if packs else matrix).astype(BF)


def weights_kernel(place_ref, w0_ref, w1_ref, w2_ref, w3_ref, down_ref, wa, wb, da, db, ready_ref):
    x, c = place_ref[0], place_ref[1]
    half = SLABS * LANES
    own = pl.multiple_of(c * half, half)
    other = pl.multiple_of((1 - c) * half, half)
    for k, w_ref in enumerate((w0_ref, w1_ref, w2_ref, w3_ref)):
        at = pl.multiple_of(((x + CHIPS - k) % CHIPS) * UNITS, 32)
        for g in range(2):
            wa[pl.ds(at + g * CHIPS * UNITS, UNITS), :] = w_ref[g * UNITS : (g + 1) * UNITS, pl.ds(own, half)]
            wb[pl.ds(at + g * CHIPS * UNITS, UNITS), :] = w_ref[g * UNITS : (g + 1) * UNITS, pl.ds(other, half)]
    for i in range(CHIPS):
        mine = pl.multiple_of((2 * i + c) * UNITS, 32)
        theirs = pl.multiple_of((2 * i + 1 - c) * UNITS, 32)
        da[i * UNITS : (i + 1) * UNITS, :] = down_ref[pl.ds(mine, UNITS), :]
        db[i * UNITS : (i + 1) * UNITS, :] = down_ref[pl.ds(theirs, UNITS), :]
    ready_ref[...] = jnp.zeros_like(ready_ref)


def unpack_kernel(in_ref, rows_ref, scale_ref):
    perm = repack_matrix(False)
    empty = jnp.zeros((GROWS, LANES), F32)
    for g in range(EXPERTS // GROUP):
        y = dot(perm, in_ref[g * GROUP : (g + 1) * GROUP].reshape(GPACK, LANES))
        first = y[:GROWS]
        gone = first > 0.5 * EMPTY
        empty = empty + jnp.where(gone, 1.0, 0.0)
        parts = [jnp.where(gone, 0.0, first)] + [y[l * GROWS : (l + 1) * GROWS] for l in range(1, SLABS)]
        rows_ref[g * GROWS : (g + 1) * GROWS, :] = jnp.concatenate([part.astype(BF) for part in parts], axis=1)
    gone = jnp.sum(empty, axis=0, keepdims=True)
    scale_ref[...] = jnp.broadcast_to(2.0 / (float(ROWS) - gone), scale_ref.shape)


def own_kernel(rows_ref, w_ref, out_ref):
    out_ref[...] = dot(rows_ref[...], w_ref[...], NT)


def other_kernel(rows_ref, w_ref, part_ref, out_ref):
    rows = ROWS // CHIPS
    for i in range(CHIPS):
        at = slice(i * rows, (i + 1) * rows)
        out_ref[i] = (part_ref[at, :] + dot(rows_ref[at, :], w_ref[...], NT)).astype(BF)


def silu_kernel(in_ref, out_ref):
    total = in_ref[0].astype(F32)
    for k in range(1, CHIPS):
        total = total + in_ref[k].astype(F32)
    half = CHIPS * UNITS
    gate, up = total[:, :half], total[:, half:]
    out_ref[...] = (gate / (1.0 + jnp.exp(-gate)) * up).astype(BF)


def down_own_kernel(hidden_ref, down_ref, out_ref, perm_ref):
    perm_ref[...] = repack_matrix(True)
    for k in range(CHIPS):
        out_ref[k] = dot(hidden_ref[k], down_ref[...])


def down_other_kernel(hidden_ref, down_ref, part_ref, perm_ref, out_ref):
    perm = perm_ref[...]
    sources = EXPERTS // CHIPS
    for k in range(CHIPS):
        rows = (part_ref[k] + dot(hidden_ref[k], down_ref[...])).astype(BF)
        for h in range(2):
            part = rows[h * GROWS : (h + 1) * GROWS]
            stack = jnp.concatenate([part[:, l * LANES : (l + 1) * LANES] for l in range(SLABS)], axis=0)
            packed = dot(perm, stack).astype(BF).reshape(GROUP, PACK, LANES)
            out_ref[k * sources + h * GROUP : k * sources + (h + 1) * GROUP] = packed


def gram_kernel(place_ref, own_ref, other_ref, scale_ref, out_ref, acc):
    x, c = place_ref[0], place_ref[1]
    half = CHIPS * UNITS
    row, col = iota((half, 2 * half), 0), iota((half, 2 * half), 1)
    even = row + UNITS * (row // UNITS)
    put_own = jnp.where(col == even + UNITS * c, 1.0, 0.0).astype(BF)
    put_other = jnp.where(col == even + UNITS * (1 - c), 1.0, 0.0).astype(BF)
    for k in range(CHIPS):
        own = own_ref[k]
        every = (dot(own, put_own) + dot(other_ref[k], put_other)).astype(BF)
        gram = dot(own, every, TN)
        acc[...] = gram if k == 0 else acc[...] + gram
    mine = acc[pl.ds(pl.multiple_of(x * UNITS, 32), UNITS), :]
    out_ref[...] = mine * scale_ref[0:1, 0:1]


def picks_kernel(ids_ref, weights_ref, out_ref):
    weights = weights_ref[...]
    shares = weights / jnp.sum(weights, axis=0, keepdims=True)
    code, _, share = codes(ids_ref[...], shares)
    code, share = code.astype(BF), share.astype(BF)
    wide = SLABS * TOK
    p = iota((wide, GPACK), 1) % PACK
    slab = (p >= CAP).astype(I32) + (p >= 2 * CAP).astype(I32) + (p >= 3 * CAP).astype(I32)
    target = (p + 4 * slab).astype(F32)
    q = iota((EXPERTS, GPACK), 1)
    for g in range(EXPERTS // GROUP):
        e = iota((EXPERTS, GPACK), 0) - g * GROUP
        spread = jnp.where((q >= e * PACK) & (q < (e + 1) * PACK), 1.0, 0.0).astype(BF)
        pick = jnp.where(dot(code, spread, TN) == target, dot(share, spread, TN), 0.0)
        out_ref[:, g * GPACK : (g + 1) * GPACK] = pick.astype(BF)


def combine_kernel(picks_ref, in_ref, out_ref):
    total = dot(picks_ref[...], in_ref[...].reshape(EXPERTS * PACK, LANES))
    out_ref[...] = jnp.concatenate(
        [total[l * TOK : (l + 1) * TOK] for l in range(SLABS)], axis=1
    ).astype(BF)


VMEM = pl.BlockSpec(memory_space=pltpu.VMEM)
SMEM = pl.BlockSpec(memory_space=pltpu.SMEM)
ANY = pl.BlockSpec(memory_space=pl.ANY)


def call(kernel, outs, ins, scratch=(), smem=False, after=(), specs=None, vmem=16, flops=0, size=0):
    read = len(ins)

    def run(*refs):
        kernel(*refs[:read], *refs[read + len(after) :])

    return pl.pallas_call(
        run,
        out_shape=outs,
        in_specs=(specs or ([SMEM] if smem else []) + [VMEM] * (len(ins) - int(smem))) + [ANY] * len(after),
        out_specs=jax.tree.map(lambda _: VMEM, outs),
        scratch_shapes=list(scratch),
        compiler_params=pltpu.CompilerParams(vmem_limit_bytes=vmem * 1024 * 1024),
        cost_estimate=pl.CostEstimate(flops=flops, bytes_accessed=size, transcendentals=0),
    )(*ins, *after)


def shape(dims, dtype=BF):
    return jax.ShapeDtypeStruct(dims, dtype)


def body(tokens, route_ids, route_weights, gate_up, down_proj):
    place = lax.axis_index("hidden")
    x, c = place // 2, place % 2
    where = jnp.stack([x, c]).astype(I32)
    half = SLABS * LANES
    wide = 2 * half
    groups = [[2 * i + j for i in range(CHIPS)] for j in range(2)]
    swap = [(i, i ^ 1) for i in range(2 * CHIPS)]

    weights = gate_up.reshape(2 * UNITS, CHIPS * wide)
    pieces = []
    for k in range(CHIPS):
        piece = lax.dynamic_slice(weights, (0, ((x + k) % CHIPS) * wide), (2 * UNITS, wide))
        if k:
            piece = lax.ppermute(piece, "hidden", [(i, (i + 2 * k) % (2 * CHIPS)) for i in range(2 * CHIPS)])
        pieces.append(piece)

    units = CHIPS * UNITS
    wa, wb, da, db, ready = call(
        weights_kernel,
        (shape((2 * units, half)),) * 2 + (shape((units, half)),) * 2 + (shape((8, LANES), F32),),
        (where, *pieces, down_proj.reshape(ROWS, half)),
        smem=True,
        size=5 * 10**6,
    )

    ids, shares = route_ids.T, route_weights.T
    outgoing = call(
        pack_kernel,
        shape((EXPERTS, PACK, LANES)),
        (tokens, ids),
        (pltpu.VMEM((TOK, half), BF), pltpu.VMEM((TOP, TOK), I32), pltpu.SemaphoreType.DMA(()), pltpu.SemaphoreType.DMA(())),
        specs=[ANY, ANY],
        vmem=56,
        flops=2 * 10**8,
        size=10**6,
    )
    arrived = lax.all_to_all(outgoing, "expert", 0, 0)
    mine, scale = call(
        unpack_kernel,
        (shape((ROWS, half)), shape((8, LANES), F32)),
        (arrived,),
        after=(ready,),
        flops=3 * 10**8,
        size=2 * 10**6,
    )
    theirs = lax.ppermute(mine, "hidden", swap)
    first = call(own_kernel, shape((ROWS, 2 * units), F32), (mine, wa), flops=6 * 10**8, size=4 * 10**6)
    part = call(
        other_kernel, shape((CHIPS, ROWS // CHIPS, 2 * units)), (theirs, wb, first), flops=6 * 10**8, size=5 * 10**6
    )
    parts = lax.all_to_all(part, "hidden", 0, 0, axis_index_groups=groups)
    hidden = call(silu_kernel, shape((ROWS // CHIPS, units)), (parts,), size=2 * 10**6)

    copies = jnp.broadcast_to(hidden[None], (CHIPS, *hidden.shape))
    own = lax.all_to_all(copies, "hidden", 0, 0, axis_index_groups=groups)
    other = lax.ppermute(own, "hidden", swap)
    first, pack = call(
        down_own_kernel,
        (shape((CHIPS, ROWS // CHIPS, half), F32), shape((GPACK, GPACK))),
        (own, da),
        flops=3 * 10**8,
        size=3 * 10**6,
    )
    returning = call(
        down_other_kernel,
        shape((EXPERTS, PACK, LANES)),
        (other, db, first, pack),
        flops=6 * 10**8,
        size=3 * 10**6,
    )
    returned = lax.all_to_all(returning, "expert", 0, 0)
    hessian = call(
        gram_kernel,
        shape((UNITS, 2 * CHIPS * UNITS), F32),
        (where, own, other, scale),
        (pltpu.VMEM((CHIPS * UNITS, 2 * CHIPS * UNITS), F32),),
        smem=True,
        flops=2 * 10**9,
        size=3 * 10**6,
    )
    picks = call(
        picks_kernel, shape((SLABS * TOK, EXPERTS * PACK)), (ids, shares), after=(returning,), flops=2 * 10**8, size=2 * 10**6
    )
    layer_out = call(combine_kernel, shape((TOK, half)), (picks, returned), flops=2 * 10**8, size=10**6)
    return layer_out, hessian[None]


def solution(mesh):
    return jax.shard_map(
        body,
        mesh=mesh,
        in_specs=(
            P("expert", "hidden"),
            P("expert", None),
            P("expert", None),
            P("expert", None, "hidden", None),
            P("expert", None, "hidden"),
        ),
        out_specs=(P("expert", "hidden"), P("expert", "hidden", None)),
        check_vma=False,
    )
```

```python
import jax
import jax.numpy as jnp
from jax import lax
from jax.experimental import pallas as pl
from jax.experimental.pallas import tpu as pltpu
from jax.sharding import PartitionSpec as P

BF = jnp.bfloat16
F32 = jnp.float32
I32 = jnp.int32

TOK = 64
TOP = 8
EXPERTS = 64
CAP = 12
LANES = 128
SLABS = 4
PACK = SLABS * CAP
GROUP = 8
GROWS = GROUP * CAP
GPACK = GROUP * PACK
CHIPS = 4
ROWS = EXPERTS * CAP
UNITS = 96
EMPTY = 64.0
NT = (((1,), (1,)), ((), ()))
TN = (((0,), (0,)), ((), ()))


def dot(a, b, dims=(((1,), (0,)), ((), ()))):
    return lax.dot_general(a, b, dims, preferred_element_type=F32)


def iota(shape, dim):
    return lax.broadcasted_iota(I32, shape, dim)


def codes(ids, shares=None):
    wide = SLABS * TOK
    copies = jnp.where((iota((TOK, wide), 1) & (TOK - 1)) == iota((TOK, wide), 0), 1.0, 0.0).astype(BF)
    ids = dot(ids.astype(F32).astype(BF), copies).astype(I32)
    if shares is not None:
        shares = dot(shares.astype(BF), copies)
    expert = iota((EXPERTS, wide), 0)
    member = jnp.zeros((EXPERTS, wide), F32)
    weight = jnp.zeros((EXPERTS, wide), F32)
    for k in range(TOP):
        hit = ids[k : k + 1, :] == expert
        member = member + jnp.where(hit, 1.0, 0.0)
        if shares is not None:
            weight = weight + jnp.where(hit, shares[k : k + 1, :], 0.0)
    row, col = iota((wide, wide), 0), iota((wide, wide), 1)
    before = jnp.where((row < TOK) & (row < (col & (TOK - 1))), 1.0, 0.0).astype(BF)
    slot = dot(member.astype(BF), before)
    slab = (iota((EXPERTS, wide), 1) >> 6).astype(F32)
    code = jnp.where(member > 0.5, slot + 16.0 * slab, -1.0)
    return code, member, weight


def pack_kernel(tok_hbm, ids_hbm, out_hbm, tok_ref, ids_ref, out_ref, tok_sem, ids_sem, out_sems):
    fetch_ids = pltpu.make_async_copy(ids_hbm, ids_ref, ids_sem)
    fetch_ids.start()
    fetch = pltpu.make_async_copy(tok_hbm, tok_ref, tok_sem)
    fetch.start()
    wide = SLABS * TOK
    p = iota((PACK, wide), 0)
    slab = (p >= CAP).astype(I32) + (p >= 2 * CAP).astype(I32) + (p >= 3 * CAP).astype(I32)
    target = (p + 4 * slab).astype(F32)
    q = iota((PACK, LANES), 0)
    first = jnp.where(q < CAP, q, -1).astype(F32)
    fetch_ids.wait()
    code, member, _ = codes(ids_ref[...])
    ones = jnp.where(iota((wide, LANES), 0) < TOK, 1.0, 0.0).astype(BF)
    count = dot(member.astype(BF), ones)
    fetch.wait()
    tok = tok_ref[...]
    slabs = jnp.concatenate([tok[:, l * LANES : (l + 1) * LANES] for l in range(SLABS)], axis=0)
    sends = []
    for c in range(EXPERTS // GROUP):
        picks = [
            jnp.where(code[e : e + 1, :] == target, 1.0, 0.0).astype(BF)
            for e in range(c * GROUP, (c + 1) * GROUP)
        ]
        rows = dot(jnp.concatenate(picks, axis=0), slabs)
        for j in range(GROUP):
            e = c * GROUP + j
            block = rows[j * PACK : (j + 1) * PACK]
            out_ref[e] = jnp.where(first >= count[e : e + 1, :], EMPTY, block).astype(BF)
        at = slice(c * GROUP, (c + 1) * GROUP)
        sends.append(pltpu.make_async_copy(out_ref.at[at], out_hbm.at[at], out_sems.at[c]))
        sends[-1].start()
    for send in sends:
        send.wait()


def repack_matrix(packs):
    loose = iota((GPACK, LANES), 0)
    slab = sum((loose >= l * GROWS).astype(I32) for l in range(1, SLABS))
    rest = loose - slab * GROWS
    source = sum((rest >= j * CAP).astype(I32) for j in range(1, GROUP))
    place = source * (PACK - CAP) + slab * CAP + rest
    parts = [
        jnp.where(place == iota((GPACK, LANES), 1) + j * LANES, 1.0, 0.0) for j in range(GPACK // LANES)
    ]
    matrix = jnp.concatenate(parts, axis=1)
    return (matrix.T if packs else matrix).astype(BF)


def weights_kernel(place_ref, w0_ref, w1_ref, w2_ref, w3_ref, down_ref, wa, wb, da, db, ready_ref, sems):
    x, c = place_ref[0], place_ref[1]
    half = SLABS * LANES
    copies = []

    def move(source, target):
        copies.append(pltpu.make_async_copy(source, target, sems.at[len(copies)]))

    for k, w_ref in enumerate((w0_ref, w1_ref, w2_ref, w3_ref)):
        at = pl.multiple_of(((x + CHIPS - k) % CHIPS) * UNITS, 32)
        base = x * (2 * half) if k == 0 else 0
        own = pl.multiple_of(base + c * half, half)
        other = pl.multiple_of(base + (1 - c) * half, half)
        for g in range(2):
            source = slice(g * UNITS, (g + 1) * UNITS)
            target = pl.ds(pl.multiple_of(at + g * CHIPS * UNITS, 32), UNITS)
            move(w_ref.at[source, pl.ds(own, half)], wa.at[target, :])
            move(w_ref.at[source, pl.ds(other, half)], wb.at[target, :])
    for i in range(CHIPS):
        mine = pl.multiple_of((2 * i + c) * UNITS, 32)
        theirs = pl.multiple_of((2 * i + 1 - c) * UNITS, 32)
        move(down_ref.at[pl.ds(mine, UNITS), :], da.at[i * UNITS : (i + 1) * UNITS, :])
        move(down_ref.at[pl.ds(theirs, UNITS), :], db.at[i * UNITS : (i + 1) * UNITS, :])
    for copy in copies:
        copy.start()
    ready_ref[...] = jnp.zeros_like(ready_ref)
    for copy in copies:
        copy.wait()


def unpack_kernel(in_ref, rows_ref, scale_ref):
    perm = repack_matrix(False)
    empty = jnp.zeros((GROWS, 2 * LANES), F32)
    for h in range(EXPERTS // GROUP // 2):
        pair = [in_ref[g * GROUP : (g + 1) * GROUP].reshape(GPACK, LANES) for g in (2 * h, 2 * h + 1)]
        y = dot(perm, jnp.concatenate(pair, axis=1))
        first = y[:GROWS]
        gone = first > 0.5 * EMPTY
        empty = empty + jnp.where(gone, 1.0, 0.0)
        parts = [jnp.where(gone, 0.0, first)] + [y[l * GROWS : (l + 1) * GROWS] for l in range(1, SLABS)]
        parts = [part.astype(BF) for part in parts]
        for j in range(2):
            at = slice((2 * h + j) * GROWS, (2 * h + j + 1) * GROWS)
            lanes = slice(j * LANES, (j + 1) * LANES)
            rows_ref[at, :] = jnp.concatenate([part[:, lanes] for part in parts], axis=1)
    gone = jnp.sum(empty[:, :LANES] + empty[:, LANES:], axis=0, keepdims=True)
    scale_ref[...] = jnp.broadcast_to(2.0 / (float(ROWS) - gone), scale_ref.shape)


def own_kernel(rows_ref, w_ref, out_ref):
    out_ref[...] = dot(rows_ref[...], w_ref[...], NT)


def other_kernel(rows_ref, w_ref, part_ref, out_ref):
    rows = ROWS // CHIPS
    for i in range(CHIPS):
        at = slice(i * rows, (i + 1) * rows)
        out_ref[i] = (part_ref[at, :] + dot(rows_ref[at, :], w_ref[...], NT)).astype(BF)


def silu_kernel(in_ref, out_ref):
    total = in_ref[0].astype(F32)
    for k in range(1, CHIPS):
        total = total + in_ref[k].astype(F32)
    half = CHIPS * UNITS
    gate, up = total[:, :half], total[:, half:]
    hidden = (gate / (1.0 + jnp.exp(-gate)) * up).astype(BF)
    for k in range(CHIPS):
        out_ref[k] = hidden


def down_own_kernel(hidden_ref, down_ref, out_ref, perm_ref):
    perm_ref[...] = repack_matrix(True)
    out_ref[...] = dot(hidden_ref[...].reshape(ROWS, CHIPS * UNITS), down_ref[...])


def down_other_kernel(hidden_ref, down_ref, part_ref, perm_ref, out_hbm, out_ref, sems):
    perm = perm_ref[...]
    rows = (part_ref[...] + dot(hidden_ref[...].reshape(ROWS, CHIPS * UNITS), down_ref[...])).astype(BF)
    sends = []
    for h in range(EXPERTS // GROUP // 2):
        stack = jnp.concatenate(
            [
                jnp.concatenate(
                    [rows[g * GROWS : (g + 1) * GROWS, l * LANES : (l + 1) * LANES] for g in (2 * h, 2 * h + 1)], axis=1
                )
                for l in range(SLABS)
            ],
            axis=0,
        )
        packed = dot(perm, stack).astype(BF)
        for j, g in enumerate((2 * h, 2 * h + 1)):
            block = packed[:, j * LANES : (j + 1) * LANES]
            out_ref[g * GROUP : (g + 1) * GROUP] = block.reshape(GROUP, PACK, LANES)
        at = slice(2 * h * GROUP, 2 * (h + 1) * GROUP)
        sends.append(pltpu.make_async_copy(out_ref.at[at], out_hbm.at[at], sems.at[h]))
        sends[-1].start()
    for send in sends:
        send.wait()


def gram_kernel(place_ref, own_ref, other_ref, scale_ref, out_ref, acc):
    x, c = place_ref[0], place_ref[1]
    half = CHIPS * UNITS
    row, col = iota((half, 2 * half), 0), iota((half, 2 * half), 1)
    even = row + UNITS * (row // UNITS)
    put_own = jnp.where(col == even + UNITS * c, 1.0, 0.0).astype(BF)
    put_other = jnp.where(col == even + UNITS * (1 - c), 1.0, 0.0).astype(BF)
    for k in range(CHIPS):
        own = own_ref[k]
        every = (dot(own, put_own) + dot(other_ref[k], put_other)).astype(BF)
        gram = dot(own, every, TN)
        acc[...] = gram if k == 0 else acc[...] + gram
    mine = acc[pl.ds(pl.multiple_of(x * UNITS, 32), UNITS), :]
    out_ref[...] = mine * scale_ref[0:1, 0:1]


def picks_kernel(ids_ref, weights_ref, out_ref):
    weights = weights_ref[...]
    shares = weights / jnp.sum(weights, axis=0, keepdims=True)
    code, _, share = codes(ids_ref[...], shares)
    code, share = code.astype(BF), share.astype(BF)
    wide = SLABS * TOK
    p = iota((wide, GPACK), 1) % PACK
    slab = (p >= CAP).astype(I32) + (p >= 2 * CAP).astype(I32) + (p >= 3 * CAP).astype(I32)
    target = (p + 4 * slab).astype(F32)
    q = iota((EXPERTS, GPACK), 1)
    for g in range(EXPERTS // GROUP):
        e = iota((EXPERTS, GPACK), 0) - g * GROUP
        spread = jnp.where((q >= e * PACK) & (q < (e + 1) * PACK), 1.0, 0.0).astype(BF)
        pick = jnp.where(dot(code, spread, TN) == target, dot(share, spread, TN), 0.0)
        out_ref[:, g * GPACK : (g + 1) * GPACK] = pick.astype(BF)


def combine_kernel(picks_ref, in_ref, out_ref):
    total = dot(picks_ref[...], in_ref[...].reshape(EXPERTS * PACK, LANES))
    out_ref[...] = jnp.concatenate(
        [total[l * TOK : (l + 1) * TOK] for l in range(SLABS)], axis=1
    ).astype(BF)


VMEM = pl.BlockSpec(memory_space=pltpu.VMEM)
SMEM = pl.BlockSpec(memory_space=pltpu.SMEM)
ANY = pl.BlockSpec(memory_space=pl.ANY)


def call(kernel, outs, ins, scratch=(), smem=False, after=(), specs=None, outs_in=None, vmem=12, flops=0, size=0):
    read = len(ins)

    def run(*refs):
        kernel(*refs[:read], *refs[read + len(after) :])

    return pl.pallas_call(
        run,
        out_shape=outs,
        in_specs=(specs or ([SMEM] if smem else []) + [VMEM] * (len(ins) - int(smem))) + [ANY] * len(after),
        out_specs=jax.tree.map(lambda _: outs_in or VMEM, outs),
        scratch_shapes=list(scratch),
        compiler_params=pltpu.CompilerParams(vmem_limit_bytes=vmem * 1024 * 1024),
        cost_estimate=pl.CostEstimate(flops=flops, bytes_accessed=size, transcendentals=0),
    )(*ins, *after)


def shape(dims, dtype=BF):
    return jax.ShapeDtypeStruct(dims, dtype)


def body(tokens, route_ids, route_weights, gate_up, down_proj):
    place = lax.axis_index("hidden")
    x, c = place // 2, place % 2
    where = jnp.stack([x, c]).astype(I32)
    half = SLABS * LANES
    wide = 2 * half
    groups = [[2 * i + j for i in range(CHIPS)] for j in range(2)]
    swap = [(i, i ^ 1) for i in range(2 * CHIPS)]

    units = CHIPS * UNITS
    weights = gate_up.reshape(2 * UNITS, CHIPS * wide)
    pieces = []
    for k in range(1, CHIPS):
        piece = lax.dynamic_slice(weights, (0, ((x + k) % CHIPS) * wide), (2 * UNITS, wide))
        pieces.append(lax.ppermute(piece, "hidden", [(i, (i + 2 * k) % (2 * CHIPS)) for i in range(2 * CHIPS)]))
    wa, wb, da, db, ready = call(
        weights_kernel,
        (shape((2 * units, half)),) * 2 + (shape((units, half)),) * 2 + (shape((8, LANES), F32),),
        (where, weights, *pieces, down_proj.reshape(ROWS, half)),
        (pltpu.SemaphoreType.DMA((6 * CHIPS,)),),
        specs=[SMEM] + [ANY] * 5,
        vmem=12,
        size=5 * 10**6,
    )

    ids, shares = route_ids.T, route_weights.T
    outgoing = call(
        pack_kernel,
        shape((EXPERTS, PACK, LANES)),
        (tokens, ids),
        (
            pltpu.VMEM((TOK, half), BF),
            pltpu.VMEM((TOP, TOK), I32),
            pltpu.VMEM((EXPERTS, PACK, LANES), BF),
            pltpu.SemaphoreType.DMA(()),
            pltpu.SemaphoreType.DMA(()),
            pltpu.SemaphoreType.DMA((EXPERTS // GROUP,)),
        ),
        specs=[ANY, ANY],
        outs_in=ANY,
        vmem=56,
        flops=2 * 10**8,
        size=10**6,
    )
    arrived = lax.all_to_all(outgoing, "expert", 0, 0)
    mine, scale = call(
        unpack_kernel,
        (shape((ROWS, half)), shape((8, LANES), F32)),
        (arrived,),
        after=(ready,),
        flops=3 * 10**8,
        size=2 * 10**6,
    )
    theirs = lax.ppermute(mine, "hidden", swap)
    first = call(own_kernel, shape((ROWS, 2 * units), F32), (mine, wa), flops=6 * 10**8, size=4 * 10**6)
    part = call(
        other_kernel, shape((CHIPS, ROWS // CHIPS, 2 * units)), (theirs, wb, first), flops=6 * 10**8, size=5 * 10**6
    )
    parts = lax.all_to_all(part, "hidden", 0, 0, axis_index_groups=groups)
    copies = call(silu_kernel, shape((CHIPS, ROWS // CHIPS, units)), (parts,), size=3 * 10**6)
    own = lax.all_to_all(copies, "hidden", 0, 0, axis_index_groups=groups)
    other = lax.ppermute(own, "hidden", swap)
    first, pack = call(
        down_own_kernel,
        (shape((ROWS, half), F32), shape((GPACK, GPACK))),
        (own, da),
        flops=3 * 10**8,
        size=3 * 10**6,
    )
    returning = call(
        down_other_kernel,
        shape((EXPERTS, PACK, LANES)),
        (other, db, first, pack),
        (pltpu.VMEM((EXPERTS, PACK, LANES), BF), pltpu.SemaphoreType.DMA((EXPERTS // GROUP // 2,))),
        outs_in=ANY,
        flops=6 * 10**8,
        size=3 * 10**6,
    )
    returned = lax.all_to_all(returning, "expert", 0, 0)
    hessian = call(
        gram_kernel,
        shape((UNITS, 2 * CHIPS * UNITS), F32),
        (where, own, other, scale),
        (pltpu.VMEM((CHIPS * UNITS, 2 * CHIPS * UNITS), F32),),
        smem=True,
        flops=2 * 10**9,
        size=3 * 10**6,
    )
    picks = call(
        picks_kernel, shape((SLABS * TOK, EXPERTS * PACK)), (ids, shares), after=(returning,), flops=2 * 10**8, size=2 * 10**6
    )
    layer_out = call(combine_kernel, shape((TOK, half)), (picks, returned), flops=2 * 10**8, size=10**6)
    return layer_out, hessian[None]


def solution(mesh):
    return jax.shard_map(
        body,
        mesh=mesh,
        in_specs=(
            P("expert", "hidden"),
            P("expert", None),
            P("expert", None),
            P("expert", None, "hidden", None),
            P("expert", None, "hidden"),
        ),
        out_specs=(P("expert", "hidden"), P("expert", "hidden", None)),
        check_vma=False,
    )
```

```python
import jax
import jax.numpy as jnp
from jax import lax
from jax.experimental import pallas as pl
from jax.experimental.pallas import tpu as pltpu
from jax.sharding import PartitionSpec as P

BF = jnp.bfloat16
F32 = jnp.float32
I32 = jnp.int32

TOK = 64
TOP = 8
EXPERTS = 64
CAP = 12
LANES = 128
SLABS = 4
PACK = SLABS * CAP
GROUP = 8
GROWS = GROUP * CAP
GPACK = GROUP * PACK
CHIPS = 4
ROWS = EXPERTS * CAP
UNITS = 96
EMPTY = 64.0
SENT = [16 * ((y + 3) % 4) + (z + 11) % 16 for y in range(4) for z in range(16)]
BACK = [16 * ((y + 2) % 4) + (z + 8) % 16 for y in range(4) for z in range(16)]
NT = (((1,), (1,)), ((), ()))
TN = (((0,), (0,)), ((), ()))


def dot(a, b, dims=(((1,), (0,)), ((), ()))):
    return lax.dot_general(a, b, dims, preferred_element_type=F32)


def iota(shape, dim):
    return lax.broadcasted_iota(I32, shape, dim)


def codes(ids, shares=None):
    wide = SLABS * TOK
    copies = jnp.where((iota((TOK, wide), 1) & (TOK - 1)) == iota((TOK, wide), 0), 1.0, 0.0).astype(BF)
    ids = dot(ids.astype(F32).astype(BF), copies).astype(I32)
    if shares is not None:
        shares = dot(shares.astype(BF), copies)
    expert = iota((EXPERTS, wide), 0)
    member = jnp.zeros((EXPERTS, wide), F32)
    weight = jnp.zeros((EXPERTS, wide), F32)
    for k in range(TOP):
        hit = ids[k : k + 1, :] == expert
        member = member + jnp.where(hit, 1.0, 0.0)
        if shares is not None:
            weight = weight + jnp.where(hit, shares[k : k + 1, :], 0.0)
    row, col = iota((wide, wide), 0), iota((wide, wide), 1)
    before = jnp.where((row < TOK) & (row < (col & (TOK - 1))), 1.0, 0.0).astype(BF)
    slot = dot(member.astype(BF), before)
    slab = (iota((EXPERTS, wide), 1) >> 6).astype(F32)
    code = jnp.where(member > 0.5, slot + 16.0 * slab, -1.0)
    return code, member, weight


def pack_kernel(tok_hbm, ids_hbm, out_hbm, tok_ref, ids_ref, out_ref, tok_sem, ids_sem, out_sems):
    fetch_ids = pltpu.make_async_copy(ids_hbm, ids_ref, ids_sem)
    fetch_ids.start()
    fetch = pltpu.make_async_copy(tok_hbm, tok_ref, tok_sem)
    fetch.start()
    wide = SLABS * TOK
    p = iota((PACK, wide), 0)
    slab = (p >= CAP).astype(I32) + (p >= 2 * CAP).astype(I32) + (p >= 3 * CAP).astype(I32)
    target = (p + 4 * slab).astype(F32)
    q = iota((PACK, LANES), 0)
    first = jnp.where(q < CAP, q, -1).astype(F32)
    fetch_ids.wait()
    code, member, _ = codes(ids_ref[...])
    ones = jnp.where(iota((wide, LANES), 0) < TOK, 1.0, 0.0).astype(BF)
    count = dot(member.astype(BF), ones)
    fetch.wait()
    tok = tok_ref[...]
    slabs = jnp.concatenate([tok[:, l * LANES : (l + 1) * LANES] for l in range(SLABS)], axis=0)
    sends = []
    for c in range(EXPERTS // GROUP):
        picks = [
            jnp.where(code[e : e + 1, :] == target, 1.0, 0.0).astype(BF)
            for e in SENT[c * GROUP : (c + 1) * GROUP]
        ]
        rows = dot(jnp.concatenate(picks, axis=0), slabs)
        for j in range(GROUP):
            e = SENT[c * GROUP + j]
            block = rows[j * PACK : (j + 1) * PACK]
            out_ref[c * GROUP + j] = jnp.where(first >= count[e : e + 1, :], EMPTY, block).astype(BF)
        at = slice(c * GROUP, (c + 1) * GROUP)
        sends.append(pltpu.make_async_copy(out_ref.at[at], out_hbm.at[at], out_sems.at[c]))
        sends[-1].start()
    for send in sends:
        send.wait()


def repack_matrix(packs):
    loose = iota((GPACK, LANES), 0)
    slab = sum((loose >= l * GROWS).astype(I32) for l in range(1, SLABS))
    rest = loose - slab * GROWS
    source = sum((rest >= j * CAP).astype(I32) for j in range(1, GROUP))
    place = source * (PACK - CAP) + slab * CAP + rest
    parts = [
        jnp.where(place == iota((GPACK, LANES), 1) + j * LANES, 1.0, 0.0) for j in range(GPACK // LANES)
    ]
    matrix = jnp.concatenate(parts, axis=1)
    return (matrix.T if packs else matrix).astype(BF)


def weights_kernel(place_ref, w0_ref, w1_ref, w2_ref, w3_ref, down_ref, wa, wb, da, db, ready_ref, sems):
    x, c = place_ref[0], place_ref[1]
    half = SLABS * LANES
    copies = []

    def move(source, target):
        copies.append(pltpu.make_async_copy(source, target, sems.at[len(copies)]))

    for k, w_ref in enumerate((w0_ref, w1_ref, w2_ref, w3_ref)):
        at = pl.multiple_of(((x + CHIPS - k) % CHIPS) * UNITS, 32)
        base = x * (2 * half) if k == 0 else 0
        own = pl.multiple_of(base + c * half, half)
        other = pl.multiple_of(base + (1 - c) * half, half)
        for g in range(2):
            source = slice(g * UNITS, (g + 1) * UNITS)
            target = pl.ds(pl.multiple_of(at + g * CHIPS * UNITS, 32), UNITS)
            move(w_ref.at[source, pl.ds(own, half)], wa.at[target, :])
            move(w_ref.at[source, pl.ds(other, half)], wb.at[target, :])
    for i in range(CHIPS):
        mine = pl.multiple_of((2 * i + c) * UNITS, 32)
        theirs = pl.multiple_of((2 * i + 1 - c) * UNITS, 32)
        move(down_ref.at[pl.ds(mine, UNITS), :], da.at[i * UNITS : (i + 1) * UNITS, :])
        move(down_ref.at[pl.ds(theirs, UNITS), :], db.at[i * UNITS : (i + 1) * UNITS, :])
    for copy in copies:
        copy.start()
    ready_ref[...] = jnp.zeros_like(ready_ref)
    for copy in copies:
        copy.wait()


def unpack_kernel(in_ref, rows_ref, scale_ref):
    perm = repack_matrix(False)
    empty = jnp.zeros((GROWS, 2 * LANES), F32)
    place = [SENT.index(source) for source in BACK]
    for h in range(EXPERTS // GROUP // 2):
        pair = [
            jnp.concatenate([in_ref[place[g * GROUP + j]] for j in range(GROUP)], axis=0) for g in (2 * h, 2 * h + 1)
        ]
        y = dot(perm, jnp.concatenate(pair, axis=1))
        first = y[:GROWS]
        gone = first > 0.5 * EMPTY
        empty = empty + jnp.where(gone, 1.0, 0.0)
        parts = [jnp.where(gone, 0.0, first)] + [y[l * GROWS : (l + 1) * GROWS] for l in range(1, SLABS)]
        parts = [part.astype(BF) for part in parts]
        for j in range(2):
            at = slice((2 * h + j) * GROWS, (2 * h + j + 1) * GROWS)
            lanes = slice(j * LANES, (j + 1) * LANES)
            rows_ref[at, :] = jnp.concatenate([part[:, lanes] for part in parts], axis=1)
    gone = jnp.sum(empty[:, :LANES] + empty[:, LANES:], axis=0, keepdims=True)
    scale_ref[...] = jnp.broadcast_to(2.0 / (float(ROWS) - gone), scale_ref.shape)


def own_kernel(rows_ref, w_ref, out_ref):
    out_ref[...] = dot(rows_ref[...], w_ref[...], NT)


def other_kernel(rows_ref, w_ref, part_ref, out_ref):
    rows = ROWS // CHIPS
    for i in range(CHIPS):
        at = slice(i * rows, (i + 1) * rows)
        out_ref[i] = (part_ref[at, :] + dot(rows_ref[at, :], w_ref[...], NT)).astype(BF)


def silu_kernel(in_ref, out_ref):
    total = in_ref[0].astype(F32)
    for k in range(1, CHIPS):
        total = total + in_ref[k].astype(F32)
    half = CHIPS * UNITS
    gate, up = total[:, :half], total[:, half:]
    hidden = (gate / (1.0 + jnp.exp(-gate)) * up).astype(BF)
    for k in range(CHIPS):
        out_ref[k] = hidden


def down_own_kernel(hidden_ref, down_ref, out_ref, perm_ref):
    perm_ref[...] = repack_matrix(True)
    out_ref[...] = dot(hidden_ref[...].reshape(ROWS, CHIPS * UNITS), down_ref[...])


def down_other_kernel(hidden_ref, down_ref, part_ref, perm_ref, out_hbm, out_ref, sems):
    perm = perm_ref[...]
    rows = (part_ref[...] + dot(hidden_ref[...].reshape(ROWS, CHIPS * UNITS), down_ref[...])).astype(BF)
    sends = []
    for h in range(EXPERTS // GROUP // 2):
        stack = jnp.concatenate(
            [
                jnp.concatenate(
                    [rows[g * GROWS : (g + 1) * GROWS, l * LANES : (l + 1) * LANES] for g in (2 * h, 2 * h + 1)], axis=1
                )
                for l in range(SLABS)
            ],
            axis=0,
        )
        packed = dot(perm, stack).astype(BF)
        for j, g in enumerate((2 * h, 2 * h + 1)):
            block = packed[:, j * LANES : (j + 1) * LANES]
            out_ref[g * GROUP : (g + 1) * GROUP] = block.reshape(GROUP, PACK, LANES)
        at = slice(2 * h * GROUP, 2 * (h + 1) * GROUP)
        sends.append(pltpu.make_async_copy(out_ref.at[at], out_hbm.at[at], sems.at[h]))
        sends[-1].start()
    for send in sends:
        send.wait()


def gram_kernel(place_ref, own_ref, other_ref, scale_ref, out_ref, acc):
    x, c = place_ref[0], place_ref[1]
    half = CHIPS * UNITS
    row, col = iota((half, 2 * half), 0), iota((half, 2 * half), 1)
    even = row + UNITS * (row // UNITS)
    put_own = jnp.where(col == even + UNITS * c, 1.0, 0.0).astype(BF)
    put_other = jnp.where(col == even + UNITS * (1 - c), 1.0, 0.0).astype(BF)
    for k in range(CHIPS):
        own = own_ref[k]
        every = (dot(own, put_own) + dot(other_ref[k], put_other)).astype(BF)
        gram = dot(own, every, TN)
        acc[...] = gram if k == 0 else acc[...] + gram
    mine = acc[pl.ds(pl.multiple_of(x * UNITS, 32), UNITS), :]
    out_ref[...] = mine * scale_ref[0:1, 0:1]


def picks_kernel(ids_ref, weights_ref, out_ref):
    weights = weights_ref[...]
    shares = weights / jnp.sum(weights, axis=0, keepdims=True)
    code, _, share = codes(ids_ref[...], shares)
    code, share = code.astype(BF), share.astype(BF)
    wide = SLABS * TOK
    p = iota((wide, GPACK), 1) % PACK
    slab = (p >= CAP).astype(I32) + (p >= 2 * CAP).astype(I32) + (p >= 3 * CAP).astype(I32)
    target = (p + 4 * slab).astype(F32)
    q = iota((EXPERTS, GPACK), 1)
    for g in range(EXPERTS // GROUP):
        e = iota((EXPERTS, GPACK), 0) - BACK[g * GROUP]
        spread = jnp.where((q >= e * PACK) & (q < (e + 1) * PACK), 1.0, 0.0).astype(BF)
        pick = jnp.where(dot(code, spread, TN) == target, dot(share, spread, TN), 0.0)
        out_ref[:, g * GPACK : (g + 1) * GPACK] = pick.astype(BF)


def combine_kernel(picks_ref, in_ref, out_ref):
    total = dot(picks_ref[...], in_ref[...].reshape(EXPERTS * PACK, LANES))
    out_ref[...] = jnp.concatenate(
        [total[l * TOK : (l + 1) * TOK] for l in range(SLABS)], axis=1
    ).astype(BF)


VMEM = pl.BlockSpec(memory_space=pltpu.VMEM)
SMEM = pl.BlockSpec(memory_space=pltpu.SMEM)
ANY = pl.BlockSpec(memory_space=pl.ANY)


def call(kernel, outs, ins, scratch=(), smem=False, after=(), specs=None, outs_in=None, vmem=12, flops=0, size=0):
    read = len(ins)

    def run(*refs):
        kernel(*refs[:read], *refs[read + len(after) :])

    return pl.pallas_call(
        run,
        out_shape=outs,
        in_specs=(specs or ([SMEM] if smem else []) + [VMEM] * (len(ins) - int(smem))) + [ANY] * len(after),
        out_specs=jax.tree.map(lambda _: outs_in or VMEM, outs),
        scratch_shapes=list(scratch),
        compiler_params=pltpu.CompilerParams(vmem_limit_bytes=vmem * 1024 * 1024),
        cost_estimate=pl.CostEstimate(flops=flops, bytes_accessed=size, transcendentals=0),
    )(*ins, *after)


def shape(dims, dtype=BF):
    return jax.ShapeDtypeStruct(dims, dtype)


def body(tokens, route_ids, route_weights, gate_up, down_proj):
    place = lax.axis_index("hidden")
    x, c = place // 2, place % 2
    where = jnp.stack([x, c]).astype(I32)
    half = SLABS * LANES
    wide = 2 * half
    groups = [[2 * i + j for i in range(CHIPS)] for j in range(2)]
    swap = [(i, i ^ 1) for i in range(2 * CHIPS)]

    units = CHIPS * UNITS
    weights = gate_up.reshape(2 * UNITS, CHIPS * wide)
    pieces = []
    for k in range(1, CHIPS):
        piece = lax.dynamic_slice(weights, (0, ((x + k) % CHIPS) * wide), (2 * UNITS, wide))
        pieces.append(lax.ppermute(piece, "hidden", [(i, (i + 2 * k) % (2 * CHIPS)) for i in range(2 * CHIPS)]))
    wa, wb, da, db, ready = call(
        weights_kernel,
        (shape((2 * units, half)),) * 2 + (shape((units, half)),) * 2 + (shape((8, LANES), F32),),
        (where, weights, *pieces, down_proj.reshape(ROWS, half)),
        (pltpu.SemaphoreType.DMA((6 * CHIPS,)),),
        specs=[SMEM] + [ANY] * 5,
        vmem=12,
        size=5 * 10**6,
    )

    ids, shares = route_ids.T, route_weights.T
    outgoing = call(
        pack_kernel,
        shape((EXPERTS, PACK, LANES)),
        (tokens, ids),
        (
            pltpu.VMEM((TOK, half), BF),
            pltpu.VMEM((TOP, TOK), I32),
            pltpu.VMEM((EXPERTS, PACK, LANES), BF),
            pltpu.SemaphoreType.DMA(()),
            pltpu.SemaphoreType.DMA(()),
            pltpu.SemaphoreType.DMA((EXPERTS // GROUP,)),
        ),
        specs=[ANY, ANY],
        outs_in=ANY,
        vmem=56,
        flops=2 * 10**8,
        size=10**6,
    )
    arrived = lax.all_to_all(outgoing, "expert", 0, 0, axis_index_groups=[SENT])
    mine, scale = call(
        unpack_kernel,
        (shape((ROWS, half)), shape((8, LANES), F32)),
        (arrived,),
        after=(ready,),
        flops=3 * 10**8,
        size=2 * 10**6,
    )
    theirs = lax.ppermute(mine, "hidden", swap)
    first = call(own_kernel, shape((ROWS, 2 * units), F32), (mine, wa), flops=6 * 10**8, size=4 * 10**6)
    part = call(
        other_kernel, shape((CHIPS, ROWS // CHIPS, 2 * units)), (theirs, wb, first), flops=6 * 10**8, size=5 * 10**6
    )
    parts = lax.all_to_all(part, "hidden", 0, 0, axis_index_groups=groups)
    copies = call(silu_kernel, shape((CHIPS, ROWS // CHIPS, units)), (parts,), size=3 * 10**6)
    own = lax.all_to_all(copies, "hidden", 0, 0, axis_index_groups=groups)
    other = lax.ppermute(own, "hidden", swap)
    first, pack = call(
        down_own_kernel,
        (shape((ROWS, half), F32), shape((GPACK, GPACK))),
        (own, da),
        flops=3 * 10**8,
        size=3 * 10**6,
    )
    returning = call(
        down_other_kernel,
        shape((EXPERTS, PACK, LANES)),
        (other, db, first, pack),
        (pltpu.VMEM((EXPERTS, PACK, LANES), BF), pltpu.SemaphoreType.DMA((EXPERTS // GROUP // 2,))),
        outs_in=ANY,
        flops=6 * 10**8,
        size=3 * 10**6,
    )
    returned = lax.all_to_all(returning, "expert", 0, 0, axis_index_groups=[BACK])
    hessian = call(
        gram_kernel,
        shape((UNITS, 2 * CHIPS * UNITS), F32),
        (where, own, other, scale),
        (pltpu.VMEM((CHIPS * UNITS, 2 * CHIPS * UNITS), F32),),
        smem=True,
        flops=2 * 10**9,
        size=3 * 10**6,
    )
    picks = call(
        picks_kernel, shape((SLABS * TOK, EXPERTS * PACK)), (ids, shares), after=(returning,), flops=2 * 10**8, size=2 * 10**6
    )
    layer_out = call(combine_kernel, shape((TOK, half)), (picks, returned), flops=2 * 10**8, size=10**6)
    return layer_out, hessian[None]


def solution(mesh):
    return jax.shard_map(
        body,
        mesh=mesh,
        in_specs=(
            P("expert", "hidden"),
            P("expert", None),
            P("expert", None),
            P("expert", None, "hidden", None),
            P("expert", None, "hidden"),
        ),
        out_specs=(P("expert", "hidden"), P("expert", "hidden", None)),
        check_vma=False,
    )
```

```python
import jax
import jax.numpy as jnp
from jax import lax
from jax.experimental import pallas as pl
from jax.experimental.pallas import tpu as pltpu
from jax.sharding import PartitionSpec as P

BF = jnp.bfloat16
F32 = jnp.float32
I32 = jnp.int32

TOK = 64
TOP = 8
EXPERTS = 64
CAP = 12
LANES = 128
SLABS = 4
PACK = SLABS * CAP
GROUP = 8
GROWS = GROUP * CAP
GPACK = GROUP * PACK
CHIPS = 4
ROWS = EXPERTS * CAP
UNITS = 96
EMPTY = 64.0
SENT = [16 * ((y + 3) % 4) + (z + 11) % 16 for y in range(4) for z in range(16)]
BACK = [16 * ((y + 2) % 4) + (z + 8) % 16 for y in range(4) for z in range(16)]
NT = (((1,), (1,)), ((), ()))
TN = (((0,), (0,)), ((), ()))


def dot(a, b, dims=(((1,), (0,)), ((), ()))):
    return lax.dot_general(a, b, dims, preferred_element_type=F32)


def iota(shape, dim):
    return lax.broadcasted_iota(I32, shape, dim)


def codes(ids, shares=None):
    wide = SLABS * TOK
    copies = jnp.where((iota((TOK, wide), 1) & (TOK - 1)) == iota((TOK, wide), 0), 1.0, 0.0).astype(BF)
    ids = dot(ids.astype(F32).astype(BF), copies).astype(I32)
    if shares is not None:
        shares = dot(shares.astype(BF), copies)
    expert = iota((EXPERTS, wide), 0)
    member = jnp.zeros((EXPERTS, wide), F32)
    weight = jnp.zeros((EXPERTS, wide), F32)
    for k in range(TOP):
        hit = ids[k : k + 1, :] == expert
        member = member + jnp.where(hit, 1.0, 0.0)
        if shares is not None:
            weight = weight + jnp.where(hit, shares[k : k + 1, :], 0.0)
    row, col = iota((wide, wide), 0), iota((wide, wide), 1)
    before = jnp.where((row < TOK) & (row < (col & (TOK - 1))), 1.0, 0.0).astype(BF)
    slot = dot(member.astype(BF), before)
    slab = (iota((EXPERTS, wide), 1) >> 6).astype(F32)
    code = jnp.where(member > 0.5, slot + 16.0 * slab, -1.0)
    return code, member, weight


def pack_kernel(tok_hbm, ids_hbm, out_hbm, tok_ref, ids_ref, out_ref, tok_sem, ids_sem, out_sems):
    fetch_ids = pltpu.make_async_copy(ids_hbm, ids_ref, ids_sem)
    fetch_ids.start()
    fetch = pltpu.make_async_copy(tok_hbm, tok_ref, tok_sem)
    fetch.start()
    p = iota((PACK, LANES), 0)
    slab = (p >= CAP).astype(I32) + (p >= 2 * CAP).astype(I32) + (p >= 3 * CAP).astype(I32)
    target = (p + 4 * slab).astype(F32)
    first = jnp.where(p < CAP, p, -1).astype(F32)
    expert, token = iota((EXPERTS, LANES), 0), iota((EXPERTS, LANES), 1)
    before = jnp.where(iota((TOK, LANES), 0) < (iota((TOK, LANES), 1) & (TOK - 1)), 1.0, 0.0).astype(BF)
    fetch_ids.wait()
    ids = ids_ref[...]
    ids = jnp.concatenate([ids, ids], axis=1)
    member = jnp.zeros((EXPERTS, LANES), F32)
    for k in range(TOP):
        member = member + jnp.where(ids[k : k + 1, :] == expert, 1.0, 0.0)
    single = member[:, :TOK].astype(BF)
    slot = dot(single, before)
    code = jnp.where(member > 0.5, slot + 16.0 * (token >> 6).astype(F32), -1.0)
    count = dot(single, jnp.ones((TOK, LANES), BF))
    fetch.wait()
    tok = tok_ref[...]
    slabs = jnp.concatenate([tok[:, l * LANES : (l + 1) * LANES] for l in range(SLABS)], axis=0)
    sends = []
    for c in range(EXPERTS // GROUP):
        picks = [
            jnp.concatenate(
                [jnp.where(code[e : e + 1, :] == target - 32.0 * i, 1.0, 0.0).astype(BF) for i in range(2)], axis=1
            )
            for e in SENT[c * GROUP : (c + 1) * GROUP]
        ]
        rows = dot(jnp.concatenate(picks, axis=0), slabs)
        for j in range(GROUP):
            e = SENT[c * GROUP + j]
            block = rows[j * PACK : (j + 1) * PACK]
            out_ref[c * GROUP + j] = jnp.where(first >= count[e : e + 1, :], EMPTY, block).astype(BF)
        at = slice(c * GROUP, (c + 1) * GROUP)
        sends.append(pltpu.make_async_copy(out_ref.at[at], out_hbm.at[at], out_sems.at[c]))
        sends[-1].start()
    for send in sends:
        send.wait()


def repack_matrix(packs):
    loose = iota((GPACK, LANES), 0)
    slab = sum((loose >= l * GROWS).astype(I32) for l in range(1, SLABS))
    rest = loose - slab * GROWS
    source = sum((rest >= j * CAP).astype(I32) for j in range(1, GROUP))
    place = source * (PACK - CAP) + slab * CAP + rest
    parts = [
        jnp.where(place == iota((GPACK, LANES), 1) + j * LANES, 1.0, 0.0) for j in range(GPACK // LANES)
    ]
    matrix = jnp.concatenate(parts, axis=1)
    return (matrix.T if packs else matrix).astype(BF)


def weights_kernel(place_ref, w0_ref, w1_ref, w2_ref, w3_ref, down_ref, wa, wb, da, db, ready_ref, sems):
    x, c = place_ref[0], place_ref[1]
    half = SLABS * LANES
    copies = []

    def move(source, target):
        copies.append(pltpu.make_async_copy(source, target, sems.at[len(copies)]))

    for k, w_ref in enumerate((w0_ref, w1_ref, w2_ref, w3_ref)):
        at = pl.multiple_of(((x + CHIPS - k) % CHIPS) * UNITS, 32)
        base = x * (2 * half) if k == 0 else 0
        own = pl.multiple_of(base + c * half, half)
        other = pl.multiple_of(base + (1 - c) * half, half)
        for g in range(2):
            source = slice(g * UNITS, (g + 1) * UNITS)
            target = pl.ds(pl.multiple_of(at + g * CHIPS * UNITS, 32), UNITS)
            move(w_ref.at[source, pl.ds(own, half)], wa.at[target, :])
            move(w_ref.at[source, pl.ds(other, half)], wb.at[target, :])
    for i in range(CHIPS):
        mine = pl.multiple_of((2 * i + c) * UNITS, 32)
        theirs = pl.multiple_of((2 * i + 1 - c) * UNITS, 32)
        move(down_ref.at[pl.ds(mine, UNITS), :], da.at[i * UNITS : (i + 1) * UNITS, :])
        move(down_ref.at[pl.ds(theirs, UNITS), :], db.at[i * UNITS : (i + 1) * UNITS, :])
    for copy in copies:
        copy.start()
    ready_ref[...] = jnp.zeros_like(ready_ref)
    for copy in copies:
        copy.wait()


def unpack_kernel(in_ref, rows_ref, scale_ref):
    perm = repack_matrix(False)
    empty = jnp.zeros((GROWS, 2 * LANES), F32)
    place = [SENT.index(source) for source in BACK]
    for h in range(EXPERTS // GROUP // 2):
        pair = [
            jnp.concatenate([in_ref[place[g * GROUP + j]] for j in range(GROUP)], axis=0) for g in (2 * h, 2 * h + 1)
        ]
        y = dot(perm, jnp.concatenate(pair, axis=1))
        first = y[:GROWS]
        gone = first > 0.5 * EMPTY
        empty = empty + jnp.where(gone, 1.0, 0.0)
        parts = [jnp.where(gone, 0.0, first)] + [y[l * GROWS : (l + 1) * GROWS] for l in range(1, SLABS)]
        parts = [part.astype(BF) for part in parts]
        for j in range(2):
            at = slice((2 * h + j) * GROWS, (2 * h + j + 1) * GROWS)
            lanes = slice(j * LANES, (j + 1) * LANES)
            rows_ref[at, :] = jnp.concatenate([part[:, lanes] for part in parts], axis=1)
    gone = jnp.sum(empty[:, :LANES] + empty[:, LANES:], axis=0, keepdims=True)
    scale_ref[...] = jnp.broadcast_to(2.0 / (float(ROWS) - gone), scale_ref.shape)


def own_kernel(rows_ref, w_ref, out_ref):
    out_ref[...] = dot(rows_ref[...], w_ref[...], NT)


def other_kernel(rows_ref, w_ref, part_ref, out_ref):
    rows = ROWS // CHIPS
    for i in range(CHIPS):
        at = slice(i * rows, (i + 1) * rows)
        out_ref[i] = (part_ref[at, :] + dot(rows_ref[at, :], w_ref[...], NT)).astype(BF)


def silu_kernel(in_ref, out_ref):
    total = in_ref[0].astype(F32)
    for k in range(1, CHIPS):
        total = total + in_ref[k].astype(F32)
    half = CHIPS * UNITS
    gate, up = total[:, :half], total[:, half:]
    hidden = (gate / (1.0 + jnp.exp(-gate)) * up).astype(BF)
    for k in range(CHIPS):
        out_ref[k] = hidden


def down_own_kernel(hidden_ref, down_ref, out_ref, perm_ref):
    perm_ref[...] = repack_matrix(True)
    out_ref[...] = dot(hidden_ref[...].reshape(ROWS, CHIPS * UNITS), down_ref[...])


def down_other_kernel(hidden_ref, down_ref, part_ref, perm_ref, out_hbm, out_ref, sems):
    perm = perm_ref[...]
    rows = (part_ref[...] + dot(hidden_ref[...].reshape(ROWS, CHIPS * UNITS), down_ref[...])).astype(BF)
    sends = []
    for h in range(EXPERTS // GROUP // 2):
        stack = jnp.concatenate(
            [
                jnp.concatenate(
                    [rows[g * GROWS : (g + 1) * GROWS, l * LANES : (l + 1) * LANES] for g in (2 * h, 2 * h + 1)], axis=1
                )
                for l in range(SLABS)
            ],
            axis=0,
        )
        packed = dot(perm, stack).astype(BF)
        for j, g in enumerate((2 * h, 2 * h + 1)):
            block = packed[:, j * LANES : (j + 1) * LANES]
            out_ref[g * GROUP : (g + 1) * GROUP] = block.reshape(GROUP, PACK, LANES)
        at = slice(2 * h * GROUP, 2 * (h + 1) * GROUP)
        sends.append(pltpu.make_async_copy(out_ref.at[at], out_hbm.at[at], sems.at[h]))
        sends[-1].start()
    for send in sends:
        send.wait()


def gram_kernel(place_ref, own_ref, other_ref, scale_ref, out_ref, acc):
    x, c = place_ref[0], place_ref[1]
    half = CHIPS * UNITS
    row, col = iota((half, 2 * half), 0), iota((half, 2 * half), 1)
    even = row + UNITS * (row // UNITS)
    put_own = jnp.where(col == even + UNITS * c, 1.0, 0.0).astype(BF)
    put_other = jnp.where(col == even + UNITS * (1 - c), 1.0, 0.0).astype(BF)
    for k in range(CHIPS):
        own = own_ref[k]
        every = (dot(own, put_own) + dot(other_ref[k], put_other)).astype(BF)
        gram = dot(own, every, TN)
        acc[...] = gram if k == 0 else acc[...] + gram
    mine = acc[pl.ds(pl.multiple_of(x * UNITS, 32), UNITS), :]
    out_ref[...] = mine * scale_ref[0:1, 0:1]


def picks_kernel(ids_ref, weights_ref, out_ref):
    weights = weights_ref[...]
    shares = weights / jnp.sum(weights, axis=0, keepdims=True)
    code, _, share = codes(ids_ref[...], shares)
    code, share = code.astype(BF), share.astype(BF)
    wide = SLABS * TOK
    p = iota((wide, GPACK), 1) % PACK
    slab = (p >= CAP).astype(I32) + (p >= 2 * CAP).astype(I32) + (p >= 3 * CAP).astype(I32)
    target = (p + 4 * slab).astype(F32)
    q = iota((EXPERTS, GPACK), 1)
    for g in range(EXPERTS // GROUP):
        e = iota((EXPERTS, GPACK), 0) - BACK[g * GROUP]
        spread = jnp.where((q >= e * PACK) & (q < (e + 1) * PACK), 1.0, 0.0).astype(BF)
        pick = jnp.where(dot(code, spread, TN) == target, dot(share, spread, TN), 0.0)
        out_ref[:, g * GPACK : (g + 1) * GPACK] = pick.astype(BF)


def combine_kernel(picks_ref, in_ref, out_ref):
    total = dot(picks_ref[...], in_ref[...].reshape(EXPERTS * PACK, LANES))
    out_ref[...] = jnp.concatenate(
        [total[l * TOK : (l + 1) * TOK] for l in range(SLABS)], axis=1
    ).astype(BF)


VMEM = pl.BlockSpec(memory_space=pltpu.VMEM)
SMEM = pl.BlockSpec(memory_space=pltpu.SMEM)
ANY = pl.BlockSpec(memory_space=pl.ANY)


def call(kernel, outs, ins, scratch=(), smem=False, after=(), specs=None, outs_in=None, vmem=12, flops=0, size=0):
    read = len(ins)

    def run(*refs):
        kernel(*refs[:read], *refs[read + len(after) :])

    return pl.pallas_call(
        run,
        out_shape=outs,
        in_specs=(specs or ([SMEM] if smem else []) + [VMEM] * (len(ins) - int(smem))) + [ANY] * len(after),
        out_specs=jax.tree.map(lambda _: outs_in or VMEM, outs),
        scratch_shapes=list(scratch),
        compiler_params=pltpu.CompilerParams(vmem_limit_bytes=vmem * 1024 * 1024),
        cost_estimate=pl.CostEstimate(flops=flops, bytes_accessed=size, transcendentals=0),
    )(*ins, *after)


def shape(dims, dtype=BF):
    return jax.ShapeDtypeStruct(dims, dtype)


def body(tokens, route_ids, route_weights, gate_up, down_proj):
    place = lax.axis_index("hidden")
    x, c = place // 2, place % 2
    where = jnp.stack([x, c]).astype(I32)
    half = SLABS * LANES
    wide = 2 * half
    groups = [[2 * i + j for i in (0, 2, 1, 3)] for j in range(2)]
    swap = [(i, i ^ 1) for i in range(2 * CHIPS)]

    units = CHIPS * UNITS
    weights = gate_up.reshape(2 * UNITS, CHIPS * wide)
    pieces = []
    for k in range(1, CHIPS):
        piece = lax.dynamic_slice(weights, (0, ((x + k) % CHIPS) * wide), (2 * UNITS, wide))
        pieces.append(lax.ppermute(piece, "hidden", [(i, (i + 2 * k) % (2 * CHIPS)) for i in range(2 * CHIPS)]))
    wa, wb, da, db, ready = call(
        weights_kernel,
        (shape((2 * units, half)),) * 2 + (shape((units, half)),) * 2 + (shape((8, LANES), F32),),
        (where, weights, *pieces, down_proj.reshape(ROWS, half)),
        (pltpu.SemaphoreType.DMA((6 * CHIPS,)),),
        specs=[SMEM] + [ANY] * 5,
        vmem=12,
        size=5 * 10**6,
    )

    ids, shares = route_ids.T, route_weights.T
    outgoing = call(
        pack_kernel,
        shape((EXPERTS, PACK, LANES)),
        (tokens, ids),
        (
            pltpu.VMEM((TOK, half), BF),
            pltpu.VMEM((TOP, TOK), I32),
            pltpu.VMEM((EXPERTS, PACK, LANES), BF),
            pltpu.SemaphoreType.DMA(()),
            pltpu.SemaphoreType.DMA(()),
            pltpu.SemaphoreType.DMA((EXPERTS // GROUP,)),
        ),
        specs=[ANY, ANY],
        outs_in=ANY,
        vmem=56,
        flops=2 * 10**8,
        size=10**6,
    )
    arrived = lax.all_to_all(outgoing, "expert", 0, 0, axis_index_groups=[SENT])
    mine, scale = call(
        unpack_kernel,
        (shape((ROWS, half)), shape((8, LANES), F32)),
        (arrived,),
        after=(ready,),
        flops=3 * 10**8,
        size=2 * 10**6,
    )
    theirs = lax.ppermute(mine, "hidden", swap)
    first = call(own_kernel, shape((ROWS, 2 * units), F32), (mine, wa), flops=6 * 10**8, size=4 * 10**6)
    part = call(
        other_kernel, shape((CHIPS, ROWS // CHIPS, 2 * units)), (theirs, wb, first), flops=6 * 10**8, size=5 * 10**6
    )
    parts = lax.all_to_all(part, "hidden", 0, 0, axis_index_groups=groups)
    copies = call(silu_kernel, shape((CHIPS, ROWS // CHIPS, units)), (parts,), size=3 * 10**6)
    own = lax.all_to_all(copies, "hidden", 0, 0, axis_index_groups=groups)
    other = lax.ppermute(own, "hidden", swap)
    first, pack = call(
        down_own_kernel,
        (shape((ROWS, half), F32), shape((GPACK, GPACK))),
        (own, da),
        flops=3 * 10**8,
        size=3 * 10**6,
    )
    returning = call(
        down_other_kernel,
        shape((EXPERTS, PACK, LANES)),
        (other, db, first, pack),
        (pltpu.VMEM((EXPERTS, PACK, LANES), BF), pltpu.SemaphoreType.DMA((EXPERTS // GROUP // 2,))),
        outs_in=ANY,
        flops=6 * 10**8,
        size=3 * 10**6,
    )
    returned = lax.all_to_all(returning, "expert", 0, 0, axis_index_groups=[BACK])
    hessian = call(
        gram_kernel,
        shape((UNITS, 2 * CHIPS * UNITS), F32),
        (where, own, other, scale),
        (pltpu.VMEM((CHIPS * UNITS, 2 * CHIPS * UNITS), F32),),
        smem=True,
        flops=2 * 10**9,
        size=3 * 10**6,
    )
    picks = call(
        picks_kernel, shape((SLABS * TOK, EXPERTS * PACK)), (ids, shares), after=(returning,), flops=2 * 10**8, size=2 * 10**6
    )
    layer_out = call(combine_kernel, shape((TOK, half)), (picks, returned), flops=2 * 10**8, size=10**6)
    return layer_out, hessian[None]


def solution(mesh):
    return jax.shard_map(
        body,
        mesh=mesh,
        in_specs=(
            P("expert", "hidden"),
            P("expert", None),
            P("expert", None),
            P("expert", None, "hidden", None),
            P("expert", None, "hidden"),
        ),
        out_specs=(P("expert", "hidden"), P("expert", "hidden", None)),
        check_vma=False,
    )
```

```python
import jax
import jax.numpy as jnp
from jax import lax
from jax.experimental import pallas as pl
from jax.experimental.pallas import tpu as pltpu
from jax.sharding import PartitionSpec as P

BF = jnp.bfloat16
F32 = jnp.float32
I32 = jnp.int32

TOK = 64
TOP = 8
EXPERTS = 64
CAP = 12
LANES = 128
SLABS = 4
PACK = SLABS * CAP
GROUP = 8
GROWS = GROUP * CAP
GPACK = GROUP * PACK
CHIPS = 4
ROWS = EXPERTS * CAP
UNITS = 96
EMPTY = 64.0
SENT = [16 * ((y + 3) % 4) + (z + 11) % 16 for y in range(4) for z in range(16)]
BACK = [16 * ((y + 2) % 4) + (z + 8) % 16 for y in range(4) for z in range(16)]
NT = (((1,), (1,)), ((), ()))
TN = (((0,), (0,)), ((), ()))


def dot(a, b, dims=(((1,), (0,)), ((), ()))):
    return lax.dot_general(a, b, dims, preferred_element_type=F32)


def iota(shape, dim):
    return lax.broadcasted_iota(I32, shape, dim)


def codes(ids, shares=None):
    wide = SLABS * TOK
    copies = jnp.where((iota((TOK, wide), 1) & (TOK - 1)) == iota((TOK, wide), 0), 1.0, 0.0).astype(BF)
    ids = dot(ids.astype(F32).astype(BF), copies).astype(I32)
    if shares is not None:
        shares = dot(shares.astype(BF), copies)
    expert = iota((EXPERTS, wide), 0)
    member = jnp.zeros((EXPERTS, wide), F32)
    weight = jnp.zeros((EXPERTS, wide), F32)
    for k in range(TOP):
        hit = ids[k : k + 1, :] == expert
        member = member + jnp.where(hit, 1.0, 0.0)
        if shares is not None:
            weight = weight + jnp.where(hit, shares[k : k + 1, :], 0.0)
    row, col = iota((wide, wide), 0), iota((wide, wide), 1)
    before = jnp.where((row < TOK) & (row < (col & (TOK - 1))), 1.0, 0.0).astype(BF)
    slot = dot(member.astype(BF), before)
    slab = (iota((EXPERTS, wide), 1) >> 6).astype(F32)
    code = jnp.where(member > 0.5, slot + 16.0 * slab, -1.0)
    return code, member, weight


def pack_kernel(tok_hbm, ids_hbm, out_hbm, tok_ref, ids_ref, out_ref, tok_sem, ids_sem, out_sems):
    fetch_ids = pltpu.make_async_copy(ids_hbm, ids_ref, ids_sem)
    fetch_ids.start()
    fetch = pltpu.make_async_copy(tok_hbm, tok_ref, tok_sem)
    fetch.start()
    p = iota((PACK, LANES), 0)
    slab = (p >= CAP).astype(I32) + (p >= 2 * CAP).astype(I32) + (p >= 3 * CAP).astype(I32)
    target = (p + 4 * slab).astype(F32)
    first = jnp.where(p < CAP, p, -1).astype(F32)
    expert, token = iota((EXPERTS, LANES), 0), iota((EXPERTS, LANES), 1)
    before = jnp.where(iota((TOK, LANES), 0) < (iota((TOK, LANES), 1) & (TOK - 1)), 1.0, 0.0).astype(BF)
    fetch_ids.wait()
    ids = ids_ref[...]
    ids = jnp.concatenate([ids, ids], axis=1)
    member = jnp.zeros((EXPERTS, LANES), F32)
    for k in range(TOP):
        member = member + jnp.where(ids[k : k + 1, :] == expert, 1.0, 0.0)
    single = member[:, :TOK].astype(BF)
    slot = dot(single, before)
    code = jnp.where(member > 0.5, slot + 16.0 * (token >> 6).astype(F32), -1.0)
    count = dot(single, jnp.ones((TOK, LANES), BF))
    fetch.wait()
    tok = tok_ref[...]
    slabs = jnp.concatenate([tok[:, l * LANES : (l + 1) * LANES] for l in range(SLABS)], axis=0)
    sends = []
    for c in range(EXPERTS // GROUP):
        picks = [
            jnp.concatenate(
                [jnp.where(code[e : e + 1, :] == target - 32.0 * i, 1.0, 0.0).astype(BF) for i in range(2)], axis=1
            )
            for e in SENT[c * GROUP : (c + 1) * GROUP]
        ]
        rows = dot(jnp.concatenate(picks, axis=0), slabs)
        for j in range(GROUP):
            e = SENT[c * GROUP + j]
            block = rows[j * PACK : (j + 1) * PACK]
            out_ref[c * GROUP + j] = jnp.where(first >= count[e : e + 1, :], EMPTY, block).astype(BF)
        at = slice(c * GROUP, (c + 1) * GROUP)
        sends.append(pltpu.make_async_copy(out_ref.at[at], out_hbm.at[at], out_sems.at[c]))
        sends[-1].start()
    for send in sends:
        send.wait()


def repack_matrix(packs):
    loose = iota((GPACK, LANES), 0)
    slab = sum((loose >= l * GROWS).astype(I32) for l in range(1, SLABS))
    rest = loose - slab * GROWS
    source = sum((rest >= j * CAP).astype(I32) for j in range(1, GROUP))
    place = source * (PACK - CAP) + slab * CAP + rest
    parts = [
        jnp.where(place == iota((GPACK, LANES), 1) + j * LANES, 1.0, 0.0) for j in range(GPACK // LANES)
    ]
    matrix = jnp.concatenate(parts, axis=1)
    return (matrix.T if packs else matrix).astype(BF)


def weights_kernel(place_ref, w0_ref, w1_ref, w2_ref, w3_ref, down_ref, wa, wb, da, db, ready_ref, sems):
    x, c = place_ref[0], place_ref[1]
    half = SLABS * LANES
    copies = []

    def move(source, target):
        copies.append(pltpu.make_async_copy(source, target, sems.at[len(copies)]))

    for k, w_ref in enumerate((w0_ref, w1_ref, w2_ref, w3_ref)):
        at = pl.multiple_of(((x + CHIPS - k) % CHIPS) * UNITS, 32)
        base = x * (2 * half) if k == 0 else 0
        own = pl.multiple_of(base + c * half, half)
        other = pl.multiple_of(base + (1 - c) * half, half)
        for g in range(2):
            source = slice(g * UNITS, (g + 1) * UNITS)
            target = pl.ds(pl.multiple_of(at + g * CHIPS * UNITS, 32), UNITS)
            move(w_ref.at[source, pl.ds(own, half)], wa.at[target, :])
            move(w_ref.at[source, pl.ds(other, half)], wb.at[target, :])
    for i in range(CHIPS):
        mine = pl.multiple_of((2 * i + c) * UNITS, 32)
        theirs = pl.multiple_of((2 * i + 1 - c) * UNITS, 32)
        move(down_ref.at[pl.ds(mine, UNITS), :], da.at[i * UNITS : (i + 1) * UNITS, :])
        move(down_ref.at[pl.ds(theirs, UNITS), :], db.at[i * UNITS : (i + 1) * UNITS, :])
    for copy in copies:
        copy.start()
    ready_ref[...] = jnp.zeros_like(ready_ref)
    for copy in copies:
        copy.wait()


def unpack_kernel(in_ref, rows_ref, scale_ref):
    perm = repack_matrix(False)
    empty = jnp.zeros((GROWS, 2 * LANES), F32)
    place = [SENT.index(source) for source in BACK]
    for h in range(EXPERTS // GROUP // 2):
        pair = [
            jnp.concatenate([in_ref[place[g * GROUP + j]] for j in range(GROUP)], axis=0) for g in (2 * h, 2 * h + 1)
        ]
        y = dot(perm, jnp.concatenate(pair, axis=1))
        first = y[:GROWS]
        gone = first > 0.5 * EMPTY
        empty = empty + jnp.where(gone, 1.0, 0.0)
        parts = [jnp.where(gone, 0.0, first)] + [y[l * GROWS : (l + 1) * GROWS] for l in range(1, SLABS)]
        parts = [part.astype(BF) for part in parts]
        for j in range(2):
            at = slice((2 * h + j) * GROWS, (2 * h + j + 1) * GROWS)
            lanes = slice(j * LANES, (j + 1) * LANES)
            rows_ref[at, :] = jnp.concatenate([part[:, lanes] for part in parts], axis=1)
    gone = jnp.sum(empty[:, :LANES] + empty[:, LANES:], axis=0, keepdims=True)
    scale_ref[...] = jnp.broadcast_to(2.0 / (float(ROWS) - gone), scale_ref.shape)


def own_kernel(rows_ref, w_ref, out_ref):
    out_ref[...] = dot(rows_ref[...], w_ref[...], NT)


def other_kernel(rows_ref, w_ref, part_ref, out_ref):
    part = (part_ref[...] + dot(rows_ref[...], w_ref[...], NT)).astype(BF)
    rows = ROWS // CHIPS
    for i in range(CHIPS):
        out_ref[i] = part[i * rows : (i + 1) * rows]


def silu_kernel(in_ref, out_ref):
    total = in_ref[0].astype(F32)
    for k in range(1, CHIPS):
        total = total + in_ref[k].astype(F32)
    half = CHIPS * UNITS
    gate, up = total[:, :half], total[:, half:]
    hidden = (gate / (1.0 + jnp.exp(-gate)) * up).astype(BF)
    for k in range(CHIPS):
        out_ref[k] = hidden


def down_own_kernel(hidden_ref, down_ref, out_ref, perm_ref):
    perm_ref[...] = repack_matrix(True)
    out_ref[...] = dot(hidden_ref[...].reshape(ROWS, CHIPS * UNITS), down_ref[...])


def down_other_kernel(hidden_ref, down_ref, part_ref, perm_ref, out_hbm, out_ref, sems):
    perm = perm_ref[...]
    rows = (part_ref[...] + dot(hidden_ref[...].reshape(ROWS, CHIPS * UNITS), down_ref[...])).astype(BF)
    sends = []
    for h in range(EXPERTS // GROUP // 2):
        stack = jnp.concatenate(
            [
                jnp.concatenate(
                    [rows[g * GROWS : (g + 1) * GROWS, l * LANES : (l + 1) * LANES] for g in (2 * h, 2 * h + 1)], axis=1
                )
                for l in range(SLABS)
            ],
            axis=0,
        )
        packed = dot(perm, stack).astype(BF)
        for j, g in enumerate((2 * h, 2 * h + 1)):
            block = packed[:, j * LANES : (j + 1) * LANES]
            out_ref[g * GROUP : (g + 1) * GROUP] = block.reshape(GROUP, PACK, LANES)
        at = slice(2 * h * GROUP, 2 * (h + 1) * GROUP)
        sends.append(pltpu.make_async_copy(out_ref.at[at], out_hbm.at[at], sems.at[h]))
        sends[-1].start()
    for send in sends:
        send.wait()


def gram_kernel(place_ref, own_ref, other_ref, scale_ref, out_ref, acc):
    x, c = place_ref[0], place_ref[1]
    half = CHIPS * UNITS
    row, col = iota((half, 2 * half), 0), iota((half, 2 * half), 1)
    even = row + UNITS * (row // UNITS)
    put_own = jnp.where(col == even + UNITS * c, 1.0, 0.0).astype(BF)
    put_other = jnp.where(col == even + UNITS * (1 - c), 1.0, 0.0).astype(BF)
    for k in range(CHIPS):
        own = own_ref[k]
        every = (dot(own, put_own) + dot(other_ref[k], put_other)).astype(BF)
        gram = dot(own, every, TN)
        acc[...] = gram if k == 0 else acc[...] + gram
    mine = acc[pl.ds(pl.multiple_of(x * UNITS, 32), UNITS), :]
    out_ref[...] = mine * scale_ref[0:1, 0:1]


def picks_kernel(ids_ref, weights_ref, out_ref):
    weights = weights_ref[...]
    shares = weights / jnp.sum(weights, axis=0, keepdims=True)
    code, _, share = codes(ids_ref[...], shares)
    code, share = code.astype(BF), share.astype(BF)
    wide = SLABS * TOK
    p = iota((wide, GPACK), 1) % PACK
    slab = (p >= CAP).astype(I32) + (p >= 2 * CAP).astype(I32) + (p >= 3 * CAP).astype(I32)
    target = (p + 4 * slab).astype(F32)
    q = iota((EXPERTS, GPACK), 1)
    for g in range(EXPERTS // GROUP):
        e = iota((EXPERTS, GPACK), 0) - BACK[g * GROUP]
        spread = jnp.where((q >= e * PACK) & (q < (e + 1) * PACK), 1.0, 0.0).astype(BF)
        pick = jnp.where(dot(code, spread, TN) == target, dot(share, spread, TN), 0.0)
        out_ref[:, g * GPACK : (g + 1) * GPACK] = pick.astype(BF)


def combine_kernel(picks_ref, in_ref, out_ref):
    total = dot(picks_ref[...], in_ref[...].reshape(EXPERTS * PACK, LANES))
    out_ref[...] = jnp.concatenate(
        [total[l * TOK : (l + 1) * TOK] for l in range(SLABS)], axis=1
    ).astype(BF)


VMEM = pl.BlockSpec(memory_space=pltpu.VMEM)
SMEM = pl.BlockSpec(memory_space=pltpu.SMEM)
ANY = pl.BlockSpec(memory_space=pl.ANY)


def call(kernel, outs, ins, scratch=(), smem=False, after=(), specs=None, outs_in=None, vmem=12, flops=0, size=0):
    read = len(ins)

    def run(*refs):
        kernel(*refs[:read], *refs[read + len(after) :])

    return pl.pallas_call(
        run,
        out_shape=outs,
        in_specs=(specs or ([SMEM] if smem else []) + [VMEM] * (len(ins) - int(smem))) + [ANY] * len(after),
        out_specs=jax.tree.map(lambda _: outs_in or VMEM, outs),
        scratch_shapes=list(scratch),
        compiler_params=pltpu.CompilerParams(vmem_limit_bytes=vmem * 1024 * 1024),
        cost_estimate=pl.CostEstimate(flops=flops, bytes_accessed=size, transcendentals=0),
    )(*ins, *after)


def shape(dims, dtype=BF):
    return jax.ShapeDtypeStruct(dims, dtype)


def body(tokens, route_ids, route_weights, gate_up, down_proj):
    place = lax.axis_index("hidden")
    x, c = place // 2, place % 2
    where = jnp.stack([x, c]).astype(I32)
    half = SLABS * LANES
    wide = 2 * half
    groups = [[2 * i + j for i in (0, 2, 1, 3)] for j in range(2)]
    swap = [(i, i ^ 1) for i in range(2 * CHIPS)]

    units = CHIPS * UNITS
    weights = gate_up.reshape(2 * UNITS, CHIPS * wide)
    pieces = []
    for k in range(1, CHIPS):
        piece = lax.dynamic_slice(weights, (0, ((x + k) % CHIPS) * wide), (2 * UNITS, wide))
        pieces.append(lax.ppermute(piece, "hidden", [(i, (i + 2 * k) % (2 * CHIPS)) for i in range(2 * CHIPS)]))
    wa, wb, da, db, ready = call(
        weights_kernel,
        (shape((2 * units, half)),) * 2 + (shape((units, half)),) * 2 + (shape((8, LANES), F32),),
        (where, weights, *pieces, down_proj.reshape(ROWS, half)),
        (pltpu.SemaphoreType.DMA((6 * CHIPS,)),),
        specs=[SMEM] + [ANY] * 5,
        vmem=12,
        size=5 * 10**6,
    )

    ids, shares = route_ids.T, route_weights.T
    outgoing = call(
        pack_kernel,
        shape((EXPERTS, PACK, LANES)),
        (tokens, ids),
        (
            pltpu.VMEM((TOK, half), BF),
            pltpu.VMEM((TOP, TOK), I32),
            pltpu.VMEM((EXPERTS, PACK, LANES), BF),
            pltpu.SemaphoreType.DMA(()),
            pltpu.SemaphoreType.DMA(()),
            pltpu.SemaphoreType.DMA((EXPERTS // GROUP,)),
        ),
        specs=[ANY, ANY],
        outs_in=ANY,
        vmem=56,
        flops=2 * 10**8,
        size=10**6,
    )
    arrived = lax.all_to_all(outgoing, "expert", 0, 0, axis_index_groups=[SENT])
    mine, scale = call(
        unpack_kernel,
        (shape((ROWS, half)), shape((8, LANES), F32)),
        (arrived,),
        after=(ready,),
        flops=3 * 10**8,
        size=2 * 10**6,
    )
    theirs = lax.ppermute(mine, "hidden", swap)
    first = call(own_kernel, shape((ROWS, 2 * units), F32), (mine, wa), flops=6 * 10**8, size=4 * 10**6)
    part = call(
        other_kernel, shape((CHIPS, ROWS // CHIPS, 2 * units)), (theirs, wb, first), flops=6 * 10**8, size=5 * 10**6
    )
    parts = lax.all_to_all(part, "hidden", 0, 0, axis_index_groups=groups)
    copies = call(silu_kernel, shape((CHIPS, ROWS // CHIPS, units)), (parts,), size=3 * 10**6)
    own = lax.all_to_all(copies, "hidden", 0, 0, axis_index_groups=groups)
    other = lax.ppermute(own, "hidden", swap)
    first, pack = call(
        down_own_kernel,
        (shape((ROWS, half), F32), shape((GPACK, GPACK))),
        (own, da),
        flops=3 * 10**8,
        size=3 * 10**6,
    )
    returning = call(
        down_other_kernel,
        shape((EXPERTS, PACK, LANES)),
        (other, db, first, pack),
        (pltpu.VMEM((EXPERTS, PACK, LANES), BF), pltpu.SemaphoreType.DMA((EXPERTS // GROUP // 2,))),
        outs_in=ANY,
        flops=6 * 10**8,
        size=3 * 10**6,
    )
    returned = lax.all_to_all(returning, "expert", 0, 0, axis_index_groups=[BACK])
    hessian = call(
        gram_kernel,
        shape((UNITS, 2 * CHIPS * UNITS), F32),
        (where, own, other, scale),
        (pltpu.VMEM((CHIPS * UNITS, 2 * CHIPS * UNITS), F32),),
        smem=True,
        flops=2 * 10**9,
        size=3 * 10**6,
    )
    picks = call(
        picks_kernel, shape((SLABS * TOK, EXPERTS * PACK)), (ids, shares), after=(returning,), flops=2 * 10**8, size=2 * 10**6
    )
    layer_out = call(combine_kernel, shape((TOK, half)), (picks, returned), flops=2 * 10**8, size=10**6)
    return layer_out, hessian[None]


def solution(mesh):
    return jax.shard_map(
        body,
        mesh=mesh,
        in_specs=(
            P("expert", "hidden"),
            P("expert", None),
            P("expert", None),
            P("expert", None, "hidden", None),
            P("expert", None, "hidden"),
        ),
        out_specs=(P("expert", "hidden"), P("expert", "hidden", None)),
        check_vma=False,
    )
```

```python
import jax
import jax.numpy as jnp
from jax import lax
from jax.experimental import pallas as pl
from jax.experimental.pallas import tpu as pltpu
from jax.sharding import PartitionSpec as P

BF = jnp.bfloat16
F32 = jnp.float32
I32 = jnp.int32

TOK = 64
TOP = 8
EXPERTS = 64
CAP = 12
LANES = 128
SLABS = 4
PACK = SLABS * CAP
GROUP = 8
GROWS = GROUP * CAP
GPACK = GROUP * PACK
CHIPS = 4
ROWS = EXPERTS * CAP
UNITS = 96
EMPTY = 64.0
SENT = [16 * ((y + 3) % 4) + (z + 11) % 16 for y in range(4) for z in range(16)]
BACK = [16 * ((y + 2) % 4) + (z + 8) % 16 for y in range(4) for z in range(16)]
NT = (((1,), (1,)), ((), ()))
TN = (((0,), (0,)), ((), ()))


def dot(a, b, dims=(((1,), (0,)), ((), ()))):
    return lax.dot_general(a, b, dims, preferred_element_type=F32)


def iota(shape, dim):
    return lax.broadcasted_iota(I32, shape, dim)


def codes(ids, shares=None):
    wide = SLABS * TOK
    copies = jnp.where((iota((TOK, wide), 1) & (TOK - 1)) == iota((TOK, wide), 0), 1.0, 0.0).astype(BF)
    ids = dot(ids.astype(F32).astype(BF), copies).astype(I32)
    if shares is not None:
        shares = dot(shares.astype(BF), copies)
    expert = iota((EXPERTS, wide), 0)
    member = jnp.zeros((EXPERTS, wide), F32)
    weight = jnp.zeros((EXPERTS, wide), F32)
    for k in range(TOP):
        hit = ids[k : k + 1, :] == expert
        member = member + jnp.where(hit, 1.0, 0.0)
        if shares is not None:
            weight = weight + jnp.where(hit, shares[k : k + 1, :], 0.0)
    row, col = iota((wide, wide), 0), iota((wide, wide), 1)
    before = jnp.where((row < TOK) & (row < (col & (TOK - 1))), 1.0, 0.0).astype(BF)
    slot = dot(member.astype(BF), before)
    slab = (iota((EXPERTS, wide), 1) >> 6).astype(F32)
    code = jnp.where(member > 0.5, slot + 16.0 * slab, -1.0)
    return code, member, weight


def pack_kernel(tok_hbm, ids_hbm, out_hbm, tok_ref, ids_ref, out_ref, tok_sem, ids_sem, out_sems):
    fetch_ids = pltpu.make_async_copy(ids_hbm, ids_ref, ids_sem)
    fetch_ids.start()
    fetch = pltpu.make_async_copy(tok_hbm, tok_ref, tok_sem)
    fetch.start()
    p = iota((PACK, LANES), 0)
    slab = (p >= CAP).astype(I32) + (p >= 2 * CAP).astype(I32) + (p >= 3 * CAP).astype(I32)
    target = (p + 4 * slab).astype(F32)
    first = jnp.where(p < CAP, p, -1).astype(F32)
    expert, token = iota((EXPERTS, LANES), 0), iota((EXPERTS, LANES), 1)
    before = jnp.where(iota((TOK, LANES), 0) < (iota((TOK, LANES), 1) & (TOK - 1)), 1.0, 0.0).astype(BF)
    fetch_ids.wait()
    ids = ids_ref[...]
    ids = jnp.concatenate([ids, ids], axis=1)
    member = jnp.zeros((EXPERTS, LANES), F32)
    for k in range(TOP):
        member = member + jnp.where(ids[k : k + 1, :] == expert, 1.0, 0.0)
    single = member[:, :TOK].astype(BF)
    slot = dot(single, before)
    code = jnp.where(member > 0.5, slot + 16.0 * (token >> 6).astype(F32), -1.0)
    count = dot(single, jnp.ones((TOK, LANES), BF))
    fetch.wait()
    tok = tok_ref[...]
    slabs = jnp.concatenate([tok[:, l * LANES : (l + 1) * LANES] for l in range(SLABS)], axis=0)
    sends = []
    step = 2 * GROUP
    for c in range(EXPERTS // step):
        picks = [
            jnp.concatenate(
                [jnp.where(code[e : e + 1, :] == target - 32.0 * i, 1.0, 0.0).astype(BF) for i in range(2)], axis=1
            )
            for e in SENT[c * step : (c + 1) * step]
        ]
        rows = dot(jnp.concatenate(picks, axis=0), slabs)
        for j in range(step):
            e = SENT[c * step + j]
            block = rows[j * PACK : (j + 1) * PACK]
            out_ref[c * step + j] = jnp.where(first >= count[e : e + 1, :], EMPTY, block).astype(BF)
        at = slice(c * step, (c + 1) * step)
        sends.append(pltpu.make_async_copy(out_ref.at[at], out_hbm.at[at], out_sems.at[c]))
        sends[-1].start()
    for send in sends:
        send.wait()


def repack_matrix(packs):
    loose = iota((GPACK, LANES), 0)
    slab = sum((loose >= l * GROWS).astype(I32) for l in range(1, SLABS))
    rest = loose - slab * GROWS
    source = sum((rest >= j * CAP).astype(I32) for j in range(1, GROUP))
    place = source * (PACK - CAP) + slab * CAP + rest
    parts = [
        jnp.where(place == iota((GPACK, LANES), 1) + j * LANES, 1.0, 0.0) for j in range(GPACK // LANES)
    ]
    matrix = jnp.concatenate(parts, axis=1)
    return (matrix.T if packs else matrix).astype(BF)


def weights_kernel(place_ref, w0_ref, w1_ref, w2_ref, w3_ref, down_ref, wa, wb, da, db, ready_ref, sems):
    x, c = place_ref[0], place_ref[1]
    half = SLABS * LANES
    copies = []

    def move(source, target):
        copies.append(pltpu.make_async_copy(source, target, sems.at[len(copies)]))

    for k, w_ref in enumerate((w0_ref, w1_ref, w2_ref, w3_ref)):
        at = pl.multiple_of(((x + CHIPS - k) % CHIPS) * UNITS, 32)
        base = x * (2 * half) if k == 0 else 0
        own = pl.multiple_of(base + c * half, half)
        other = pl.multiple_of(base + (1 - c) * half, half)
        for g in range(2):
            source = slice(g * UNITS, (g + 1) * UNITS)
            target = pl.ds(pl.multiple_of(at + g * CHIPS * UNITS, 32), UNITS)
            move(w_ref.at[source, pl.ds(own, half)], wa.at[target, :])
            move(w_ref.at[source, pl.ds(other, half)], wb.at[target, :])
    for i in range(CHIPS):
        mine = pl.multiple_of((2 * i + c) * UNITS, 32)
        theirs = pl.multiple_of((2 * i + 1 - c) * UNITS, 32)
        move(down_ref.at[pl.ds(mine, UNITS), :], da.at[i * UNITS : (i + 1) * UNITS, :])
        move(down_ref.at[pl.ds(theirs, UNITS), :], db.at[i * UNITS : (i + 1) * UNITS, :])
    for copy in copies:
        copy.start()
    ready_ref[...] = jnp.zeros_like(ready_ref)
    for copy in copies:
        copy.wait()


def unpack_kernel(in_ref, rows_ref, scale_ref):
    perm = repack_matrix(False)
    empty = jnp.zeros((GROWS, 2 * LANES), F32)
    place = [SENT.index(source) for source in BACK]
    for h in range(EXPERTS // GROUP // 2):
        pair = [
            jnp.concatenate([in_ref[place[g * GROUP + j]] for j in range(GROUP)], axis=0) for g in (2 * h, 2 * h + 1)
        ]
        y = dot(perm, jnp.concatenate(pair, axis=1))
        first = y[:GROWS]
        gone = first > 0.5 * EMPTY
        empty = empty + jnp.where(gone, 1.0, 0.0)
        parts = [jnp.where(gone, 0.0, first)] + [y[l * GROWS : (l + 1) * GROWS] for l in range(1, SLABS)]
        parts = [part.astype(BF) for part in parts]
        for j in range(2):
            at = slice((2 * h + j) * GROWS, (2 * h + j + 1) * GROWS)
            lanes = slice(j * LANES, (j + 1) * LANES)
            rows_ref[at, :] = jnp.concatenate([part[:, lanes] for part in parts], axis=1)
    gone = jnp.sum(empty[:, :LANES] + empty[:, LANES:], axis=0, keepdims=True)
    scale_ref[...] = jnp.broadcast_to(2.0 / (float(ROWS) - gone), scale_ref.shape)


def own_kernel(rows_ref, w_ref, out_ref):
    out_ref[...] = dot(rows_ref[...], w_ref[...], NT)


def other_kernel(rows_ref, w_ref, part_ref, out_ref):
    part = (part_ref[...] + dot(rows_ref[...], w_ref[...], NT)).astype(BF)
    rows = ROWS // CHIPS
    for i in range(CHIPS):
        out_ref[i] = part[i * rows : (i + 1) * rows]


def silu_kernel(in_ref, out_ref):
    total = in_ref[0].astype(F32)
    for k in range(1, CHIPS):
        total = total + in_ref[k].astype(F32)
    half = CHIPS * UNITS
    gate, up = total[:, :half], total[:, half:]
    hidden = (gate / (1.0 + jnp.exp(-gate)) * up).astype(BF)
    for k in range(CHIPS):
        out_ref[k] = hidden


def down_own_kernel(hidden_ref, down_ref, out_ref, perm_ref):
    perm_ref[...] = repack_matrix(True)
    out_ref[...] = dot(hidden_ref[...].reshape(ROWS, CHIPS * UNITS), down_ref[...])


def down_other_kernel(hidden_ref, down_ref, part_ref, perm_ref, out_hbm, out_ref, sems):
    perm = perm_ref[...]
    rows = (part_ref[...] + dot(hidden_ref[...].reshape(ROWS, CHIPS * UNITS), down_ref[...])).astype(BF)
    sends = []
    for h in range(EXPERTS // GROUP // 2):
        stack = jnp.concatenate(
            [
                jnp.concatenate(
                    [rows[g * GROWS : (g + 1) * GROWS, l * LANES : (l + 1) * LANES] for g in (2 * h, 2 * h + 1)], axis=1
                )
                for l in range(SLABS)
            ],
            axis=0,
        )
        packed = dot(perm, stack).astype(BF)
        for j, g in enumerate((2 * h, 2 * h + 1)):
            block = packed[:, j * LANES : (j + 1) * LANES]
            out_ref[g * GROUP : (g + 1) * GROUP] = block.reshape(GROUP, PACK, LANES)
        at = slice(2 * h * GROUP, 2 * (h + 1) * GROUP)
        sends.append(pltpu.make_async_copy(out_ref.at[at], out_hbm.at[at], sems.at[h]))
        sends[-1].start()
    for send in sends:
        send.wait()


def gram_kernel(place_ref, own_ref, other_ref, scale_ref, out_ref, acc):
    x, c = place_ref[0], place_ref[1]
    half = CHIPS * UNITS
    row, col = iota((half, 2 * half), 0), iota((half, 2 * half), 1)
    even = row + UNITS * (row // UNITS)
    put_own = jnp.where(col == even + UNITS * c, 1.0, 0.0).astype(BF)
    put_other = jnp.where(col == even + UNITS * (1 - c), 1.0, 0.0).astype(BF)
    for k in range(CHIPS):
        own = own_ref[k]
        every = (dot(own, put_own) + dot(other_ref[k], put_other)).astype(BF)
        gram = dot(own, every, TN)
        acc[...] = gram if k == 0 else acc[...] + gram
    mine = acc[pl.ds(pl.multiple_of(x * UNITS, 32), UNITS), :]
    out_ref[...] = mine * scale_ref[0:1, 0:1]


def picks_kernel(ids_ref, weights_ref, out_ref):
    weights = weights_ref[...]
    shares = weights / jnp.sum(weights, axis=0, keepdims=True)
    code, _, share = codes(ids_ref[...], shares)
    code, share = code.astype(BF), share.astype(BF)
    wide = SLABS * TOK
    p = iota((wide, GPACK), 1) % PACK
    slab = (p >= CAP).astype(I32) + (p >= 2 * CAP).astype(I32) + (p >= 3 * CAP).astype(I32)
    target = (p + 4 * slab).astype(F32)
    q = iota((EXPERTS, GPACK), 1)
    for g in range(EXPERTS // GROUP):
        e = iota((EXPERTS, GPACK), 0) - BACK[g * GROUP]
        spread = jnp.where((q >= e * PACK) & (q < (e + 1) * PACK), 1.0, 0.0).astype(BF)
        pick = jnp.where(dot(code, spread, TN) == target, dot(share, spread, TN), 0.0)
        out_ref[:, g * GPACK : (g + 1) * GPACK] = pick.astype(BF)


def combine_kernel(picks_ref, in_ref, out_ref):
    total = dot(picks_ref[...], in_ref[...].reshape(EXPERTS * PACK, LANES))
    out_ref[...] = jnp.concatenate(
        [total[l * TOK : (l + 1) * TOK] for l in range(SLABS)], axis=1
    ).astype(BF)


VMEM = pl.BlockSpec(memory_space=pltpu.VMEM)
SMEM = pl.BlockSpec(memory_space=pltpu.SMEM)
ANY = pl.BlockSpec(memory_space=pl.ANY)


def call(kernel, outs, ins, scratch=(), smem=False, after=(), specs=None, outs_in=None, vmem=12, flops=0, size=0):
    read = len(ins)

    def run(*refs):
        kernel(*refs[:read], *refs[read + len(after) :])

    return pl.pallas_call(
        run,
        out_shape=outs,
        in_specs=(specs or ([SMEM] if smem else []) + [VMEM] * (len(ins) - int(smem))) + [ANY] * len(after),
        out_specs=jax.tree.map(lambda _: outs_in or VMEM, outs),
        scratch_shapes=list(scratch),
        compiler_params=pltpu.CompilerParams(vmem_limit_bytes=vmem * 1024 * 1024),
        cost_estimate=pl.CostEstimate(flops=flops, bytes_accessed=size, transcendentals=0),
    )(*ins, *after)


def shape(dims, dtype=BF):
    return jax.ShapeDtypeStruct(dims, dtype)


def body(tokens, route_ids, route_weights, gate_up, down_proj):
    place = lax.axis_index("hidden")
    x, c = place // 2, place % 2
    where = jnp.stack([x, c]).astype(I32)
    half = SLABS * LANES
    wide = 2 * half
    groups = [[2 * i + j for i in (0, 2, 1, 3)] for j in range(2)]
    swap = [(i, i ^ 1) for i in range(2 * CHIPS)]

    units = CHIPS * UNITS
    weights = gate_up.reshape(2 * UNITS, CHIPS * wide)
    pieces = []
    for k in range(1, CHIPS):
        piece = lax.dynamic_slice(weights, (0, ((x + k) % CHIPS) * wide), (2 * UNITS, wide))
        pieces.append(lax.ppermute(piece, "hidden", [(i, (i + 2 * k) % (2 * CHIPS)) for i in range(2 * CHIPS)]))
    wa, wb, da, db, ready = call(
        weights_kernel,
        (shape((2 * units, half)),) * 2 + (shape((units, half)),) * 2 + (shape((8, LANES), F32),),
        (where, weights, *pieces, down_proj.reshape(ROWS, half)),
        (pltpu.SemaphoreType.DMA((6 * CHIPS,)),),
        specs=[SMEM] + [ANY] * 5,
        vmem=12,
        size=5 * 10**6,
    )

    ids, shares = route_ids.T, route_weights.T
    outgoing = call(
        pack_kernel,
        shape((EXPERTS, PACK, LANES)),
        (tokens, ids),
        (
            pltpu.VMEM((TOK, half), BF),
            pltpu.VMEM((TOP, TOK), I32),
            pltpu.VMEM((EXPERTS, PACK, LANES), BF),
            pltpu.SemaphoreType.DMA(()),
            pltpu.SemaphoreType.DMA(()),
            pltpu.SemaphoreType.DMA((EXPERTS // GROUP,)),
        ),
        specs=[ANY, ANY],
        outs_in=ANY,
        vmem=56,
        flops=2 * 10**8,
        size=10**6,
    )
    arrived = lax.all_to_all(outgoing, "expert", 0, 0, axis_index_groups=[SENT])
    mine, scale = call(
        unpack_kernel,
        (shape((ROWS, half)), shape((8, LANES), F32)),
        (arrived,),
        after=(ready,),
        flops=3 * 10**8,
        size=2 * 10**6,
    )
    theirs = lax.ppermute(mine, "hidden", swap)
    first = call(own_kernel, shape((ROWS, 2 * units), F32), (mine, wa), flops=6 * 10**8, size=4 * 10**6)
    part = call(
        other_kernel, shape((CHIPS, ROWS // CHIPS, 2 * units)), (theirs, wb, first), flops=6 * 10**8, size=5 * 10**6
    )
    parts = lax.all_to_all(part, "hidden", 0, 0, axis_index_groups=groups)
    copies = call(silu_kernel, shape((CHIPS, ROWS // CHIPS, units)), (parts,), size=3 * 10**6)
    own = lax.all_to_all(copies, "hidden", 0, 0, axis_index_groups=groups)
    other = lax.ppermute(own, "hidden", swap)
    first, pack = call(
        down_own_kernel,
        (shape((ROWS, half), F32), shape((GPACK, GPACK))),
        (own, da),
        flops=3 * 10**8,
        size=3 * 10**6,
    )
    returning = call(
        down_other_kernel,
        shape((EXPERTS, PACK, LANES)),
        (other, db, first, pack),
        (pltpu.VMEM((EXPERTS, PACK, LANES), BF), pltpu.SemaphoreType.DMA((EXPERTS // GROUP // 2,))),
        outs_in=ANY,
        flops=6 * 10**8,
        size=3 * 10**6,
    )
    returned = lax.all_to_all(returning, "expert", 0, 0, axis_index_groups=[BACK])
    hessian = call(
        gram_kernel,
        shape((UNITS, 2 * CHIPS * UNITS), F32),
        (where, own, other, scale),
        (pltpu.VMEM((CHIPS * UNITS, 2 * CHIPS * UNITS), F32),),
        smem=True,
        flops=2 * 10**9,
        size=3 * 10**6,
    )
    picks = call(
        picks_kernel, shape((SLABS * TOK, EXPERTS * PACK)), (ids, shares), after=(returning,), flops=2 * 10**8, size=2 * 10**6
    )
    layer_out = call(combine_kernel, shape((TOK, half)), (picks, returned), flops=2 * 10**8, size=10**6)
    return layer_out, hessian[None]


def solution(mesh):
    return jax.shard_map(
        body,
        mesh=mesh,
        in_specs=(
            P("expert", "hidden"),
            P("expert", None),
            P("expert", None),
            P("expert", None, "hidden", None),
            P("expert", None, "hidden"),
        ),
        out_specs=(P("expert", "hidden"), P("expert", "hidden", None)),
        check_vma=False,
    )
```
